32 devices in a mesh: slab: 8 (over z, x), img: 4 (over y, core).
Axes of the slice: x: 2, y: 2, z: 4, core: 2. Of those that a mesh axis runs over, the one named last changes fastest.
Arguments:
- images: bfloat16 [4096, 2, 4, 512], P(('slab', 'img')), may hold values from -6 to 6
- pose_bins: int32 [4096], P(('slab', 'img')), may hold values from 0 to 511, as said below
- labels: int32 [4096], P(('slab', 'img')), may hold values from 0 to 1
- defocus: bfloat16 [4096], P(('slab', 'img')), may hold values from 0.5 to 2
Outputs:
- maps: float32 [4, 1024, 2, 32], P('img', 'slab')
The draws below stay inside these ranges and needn't reach their ends.
Inputs may be any that keep to these rules, and one draw needn't show every extreme that they name: With owner = (pose_bins // 16) // 4: among the 128 images of one device (aligned blocks in order), no owner is named more than 32 times, and one owner, the same for all blocks, is named exactly 32 times in every block.
All inputs are finite; a program needn't handle non-finite values.
Results may differ from the reference program's by a relative error of at most 0.025.
Values may be sent and summed in bfloat16 or wider, within the bound.
No kernel may reach another device: no remote copies, remote signals or barrier semaphores. Data moves between devices by JAX's collectives and lax.ppermute only.
A program may use at most 64 MiB of HBM per device.

```python
import math
import jax
import jax.numpy as jnp
from jax import lax

NX = 512
KY = 4
CLASSES = 2
ZDEV = 4
ZBINS = 4
XBINS = 4
IMG_DEV = 128
NZ = 32
IMAGES = 4096


def draw_pose_bins(key, part):
    owners = NZ // ZDEV
    capacity = 2 * IMG_DEV // owners
    slot_grand_count = owners * capacity
    level_key, hot_key, block_base = jax.random.split(key, 3)
    load_levels = jax.random.randint(level_key, (owners,), 0, 4)
    busiest_bins = jax.random.randint(hot_key, (), 0, owners)
    slot_holder_rank = jnp.arange(slot_grand_count, dtype=jnp.int32) // capacity

    def one_block(block_index):
        random_keys = jax.random.split(jax.random.fold_in(block_base, block_index), 6)
        popular_bin_holder = jax.random.randint(random_keys[0], (), 0, owners)
        random_jitter = jax.random.randint(random_keys[1], (slot_grand_count,), 0, 64)
        extra_score = jnp.where((slot_holder_rank == busiest_bins) | (slot_holder_rank == popular_bin_holder), 1000, 0)
        bin_score = (load_levels[slot_holder_rank] * 48 + random_jitter + extra_score) * slot_grand_count + jax.random.permutation(random_keys[2], slot_grand_count)
        ranked = lax.top_k(bin_score, IMG_DEV)[1]
        picked = ranked[jax.random.permutation(random_keys[3], IMG_DEV)]
        owner_of = picked // capacity
        planes = owner_of * ZDEV + jax.random.randint(random_keys[4], (IMG_DEV,), 0, ZDEV)
        remainder = jax.random.randint(random_keys[5], (IMG_DEV,), 0, ZBINS * XBINS)
        return (planes * (ZBINS * XBINS) + remainder).astype(jnp.int32)
    return jax.vmap(one_block)(jnp.arange(IMAGES // IMG_DEV, dtype=jnp.int32)).reshape(IMAGES)


def touch_ends(drawn, rng, smallest, largest):
    longest = drawn.shape.index(max(drawn.shape))
    spots = []
    for shift in (0, 1):
        where = [jax.random.randint(jax.random.fold_in(rng, axis), (), 0, length) for axis, length in enumerate(drawn.shape)]
        where[longest] = (where[longest] + shift) % drawn.shape[longest]
        spots.append(tuple(where))
    return drawn.at[spots[0]].set(smallest).at[spots[1]].set(largest)


def block_scale(rng, extent, cuts, least, top_value):
    def one(dim, parts):
        steps = jax.random.uniform(jax.random.fold_in(jax.random.fold_in(rng, 6), dim), (parts,), jnp.float32, least / len(cuts), top_value / len(cuts))
        return jnp.repeat(jnp.exp(steps), extent[dim] // parts).reshape((-1,) + (1,) * (len(extent) - dim - 1))

    level = one(*cuts[0])
    for cut in cuts[1:]:
        level = level * one(*cut)
    return level


def gaussian(own_key, extent, width, limit, cuts=(), kind=jnp.bfloat16):
    level = block_scale(own_key, extent, cuts, -0.22, 0.18) if cuts else 1.0
    values = jax.random.normal(own_key, extent, jnp.float32) * width * level
    return jnp.minimum(jnp.maximum(values, -limit), limit).astype(kind)


def setup_inputs(seed: int = 0) -> dict:
    streams_of = jax.random.split(jax.random.key(seed), 5)
    images = gaussian(streams_of[0], (IMAGES, 2, KY, NX), 1.0, 6.0, ((0, 32),))
    pose_bins = draw_pose_bins(jax.random.fold_in(streams_of[4], 71), 0)
    labels = touch_ends(jax.random.randint(streams_of[2], (IMAGES,), 0, CLASSES), jax.random.fold_in(streams_of[2], 1), 0, CLASSES - 1).astype(jnp.int32)
    defocus = jnp.clip(jnp.exp(math.log(2.0) - 1.3862944 * jax.random.uniform(streams_of[3], (IMAGES,), jnp.float32) ** block_scale(streams_of[3], (IMAGES,), ((0, 32),), -0.2, 0.2)), 0.5, 2.0).astype(jnp.bfloat16)
    return dict(images=images, pose_bins=pose_bins, labels=labels, defocus=defocus)


def lanczos_taps(fraction):
    offsets = jnp.arange(8, dtype=jnp.float32) - 3.0
    distance = offsets[None, :] - fraction[:, None]
    kernel = jnp.sinc(distance) * jnp.sinc(distance / 4.0)
    return (kernel / lax.optimization_barrier(jnp.sum(kernel, axis=-1, keepdims=True))).astype(jnp.bfloat16)

def ctf_weights(defocus, ky_rows, x_width):
    x_index = jnp.arange(x_width, dtype=jnp.int32)
    signed = (x_index + x_width // 2) % x_width - x_width // 2
    y_index = jnp.arange(ky_rows, dtype=jnp.int32) + 1
    radius = (y_index[:, None] * y_index[:, None] + signed[None, :] * signed[None, :]).astype(jnp.float32)
    radius = radius / float(x_width * x_width)
    phase_arg = 400.0 * math.pi * defocus.astype(jnp.float32)[:, None, None] * radius[None]
    return jnp.sin(phase_arg + 0.1)

def settle(values):
    return lax.optimization_barrier(values.astype(jnp.bfloat16)).astype(jnp.float32)

def reference(images, pose_bins, labels, defocus):
    per_pose = ZBINS * XBINS
    block_size = math.gcd(IMAGES, 1024)
    num_blocks = IMAGES // block_size

    def add_block(volume, block_index):
        first_row = block_index * block_size
        rows_now = lax.dynamic_slice_in_dim(images, first_row, block_size, 0)
        pose_rows = lax.dynamic_slice_in_dim(pose_bins, first_row, block_size, 0)
        label_rows = lax.dynamic_slice_in_dim(labels, first_row, block_size, 0)
        focus_rows = lax.dynamic_slice_in_dim(defocus, first_row, block_size, 0)
        weighted = settle(ctf_weights(focus_rows, KY, NX)[:, None] * rows_now.astype(jnp.float32))
        x_taps = lax.optimization_barrier(lanczos_taps(((pose_rows % XBINS).astype(jnp.float32) + 0.5) / XBINS)).astype(jnp.float32)
        summed = jnp.zeros(weighted.shape, jnp.float32)
        for tap_no in range(8):
            summed = summed + x_taps[:, tap_no][:, None, None, None] * jnp.roll(weighted, tap_no - 3, axis=3)
        placed = settle(summed)
        begin_plane = pose_rows // per_pose
        zbin_frac = (pose_rows // XBINS % ZBINS).astype(jnp.float32)
        z_taps = lax.optimization_barrier(lanczos_taps((zbin_frac + 0.5) / ZBINS)).astype(jnp.float32)
        planes = (begin_plane[:, None] + jnp.arange(8, dtype=jnp.int32)[None, :]) % NZ
        dest_rows = (label_rows[:, None] * NZ + planes).reshape(-1)
        contrib = (z_taps[:, :, None] * placed.reshape(block_size, 1, -1)).reshape(block_size * 8, -1)
        return (volume.at[dest_rows].add(contrib), None)
    volume = jnp.zeros((CLASSES * NZ, 2 * KY * NX), jnp.float32)
    volume, _ = lax.scan(add_block, volume, jnp.arange(num_blocks, dtype=jnp.int32))
    volume = volume.reshape(CLASSES, NZ, 2, KY, NX)
    cplx_vol = volume[:, :, 0] + 1j * volume[:, :, 1]
    spatial = jnp.fft.ifft2(cplx_vol, axes=(1, 3)) * (NZ * NX)
    stacked = jnp.stack([jnp.real(spatial), jnp.imag(spatial)], axis=0)
    stacked = jnp.transpose(stacked, (3, 1, 4, 0, 2)).reshape(KY, CLASSES * NX, 2, NZ)
    return (stacked * (2.5 / math.sqrt(IMAGES * NX))).astype(jnp.float32)
```

```python
import functools
import math

import jax
import jax.numpy as jnp
import numpy as np
from jax import lax
from jax.experimental import pallas as pl
from jax.experimental.pallas import tpu as pltpu
from jax.sharding import PartitionSpec as P

NX = 512
KY = 4
CLASSES = 2
ZBINS = 4
XBINS = 4
TAPS = 8
LANES = 128
QUARTERS = NX // LANES
PLANES = 32
CHUNKS = 4
UNROLL = 8
ROWS = QUARTERS * KY
bf16, f32 = jnp.bfloat16, jnp.float32


def lanczos_taps(num_bins):
    fraction = (np.arange(num_bins, dtype=np.float32) + np.float32(0.5)) / np.float32(num_bins)
    distance = (np.arange(TAPS, dtype=np.float32) - np.float32(3.0))[None, :] - fraction[:, None]
    kernel = (np.sinc(distance) * np.sinc(distance / np.float32(4.0))).astype(np.float32)
    return (kernel / kernel.sum(-1, keepdims=True)).astype(jnp.bfloat16).astype(np.float32)


def turns_per_defocus():
    x = np.arange(NX)
    signed = (x + NX // 2) % NX - NX // 2
    y = np.arange(KY) + 1
    radius = 200.0 * (y[:, None] ** 2 + signed[None, :] ** 2) / NX**2
    table = radius.reshape(KY, QUARTERS, LANES).transpose(1, 0, 2).reshape(ROWS, LANES)
    return table.astype(np.float32)


def shift_table():
    taps = lanczos_taps(XBINS)
    out = np.zeros((XBINS, NX, NX), np.float32)
    x_out = np.arange(NX)
    for tap in range(TAPS):
        out[:, (x_out - tap + 3) % NX, x_out] += taps[:, tap][:, None]
    out = out.reshape(XBINS, NX, LANES, QUARTERS).transpose(0, 1, 3, 2)
    return out.reshape(XBINS * NX, NX).astype(jnp.bfloat16)


def fourier_table():
    m, k = np.arange(LANES)[:, None], np.arange(LANES)[None, :]
    blocks = []
    for p in range(QUARTERS):
        angle = 2.0 * np.pi * (((4 * m + p) * k) % NX) / NX
        cos, sin = np.cos(angle), np.sin(angle)
        blocks.append(np.block([[cos, sin], [-sin, cos]]))
    return np.concatenate(blocks).astype(jnp.bfloat16)


def sine_coefficients(terms=5):
    f = 0.5 * np.cos(np.linspace(0.0, np.pi / 2, 4001))
    basis = f[:, None] ** (2 * np.arange(terms) + 1)
    return np.linalg.lstsq(basis, np.sin(2 * np.pi * f), rcond=None)[0].astype(np.float32)


def device_bits():
    slab, img = lax.axis_index("slab"), lax.axis_index("img")
    return img // 2, slab % 2, slab // 2 % 2, slab // 4


def transform(get_rows, spread, table_s, table_f, v_ref, put):
    cz = CLASSES * PLANES
    for y in range(2):
        for r in range(2):
            part = jnp.dot(spread, get_rows(r, y), preferred_element_type=f32).astype(bf16)
            at = (r * 2 + y) * cz
            for b in range(XBINS):
                v_ref[at : at + cz, b * NX : (b + 1) * NX] = part[b * cz : (b + 1) * cz]
    placed = jnp.dot(v_ref[...], table_s(), preferred_element_type=f32).astype(bf16)
    real, imag = placed[: 2 * cz], placed[2 * cz :]
    sums = []
    for p in range(QUARTERS):
        lanes = slice(p * LANES, (p + 1) * LANES)
        both = jnp.concatenate([real[:, lanes], imag[:, lanes]], axis=1)
        sums.append(jnp.dot(both, table_f(p), preferred_element_type=f32))
    g0, g1, g2, g3 = sums
    a, b, c, d = g0 + g2, g0 - g2, g1 + g3, g1 - g3
    turned = jnp.concatenate([-d[:, LANES:], d[:, :LANES]], axis=1)
    quarters = (a + c, b + turned, a - c, b - turned)
    for y in range(2):
        for cls in range(CLASSES):
            at = (y * CLASSES + cls) * PLANES
            for q in range(QUARTERS):
                put(y, cls, q, quarters[q][at : at + PLANES].astype(bf16))


def spread_matrix(pose, label, planes, first_plane):
    per_pose = ZBINS * XBINS
    taps = lanczos_taps(ZBINS)
    start, zbin, xbin = pose // per_pose, pose // XBINS % ZBINS, pose % XBINS
    shape = (XBINS * CLASSES * PLANES, pose.shape[1])
    row = lax.broadcasted_iota(jnp.int32, shape, 0)
    tap = (first_plane + row % PLANES - start + planes) % planes
    tap = jnp.where(row // PLANES == xbin * CLASSES + label, tap, -1)
    out = jnp.zeros(shape, f32)
    for t in range(TAPS):
        weight = jnp.full(pose.shape, float(taps[0, t]), f32)
        for z in range(1, ZBINS):
            weight = jnp.where(zbin == z, float(taps[z, t]), weight)
        out = jnp.where(tap == t, weight, out)
    return out.astype(bf16)


def place(out_ref):
    my_y, my_x, my_z, my_class = device_bits()

    def put(y, cls, q, value):
        index = ((q % 2) ^ my_x) * 8 + (y ^ my_y) * 4 + (cls ^ my_class) * 2 + ((q // 2) ^ my_z)
        out_ref[index] = value

    return put


def first_kernel(planes, x_hbm, focus_hbm, pose_hbm, label_hbm, turns_hbm, s_hbm, f_hbm,
                 out_ref, rows_ref, spread_ref, s_ref, f_ref,
                 x_ref, focus_ref, pose_ref, label_ref, turns_ref, wide_ref, w_ref, v_ref, sems):
    number = wide_ref.shape[0]
    chunk = x_ref.shape[0] // CHUNKS

    def copy(source, target, at):
        made = pltpu.make_async_copy(source, target, sems.at[at])
        made.start()
        return made

    small = [
        copy(source, target, at)
        for at, (source, target) in enumerate(
            ((focus_hbm, focus_ref), (turns_hbm, turns_ref), (pose_hbm, pose_ref), (label_hbm, label_ref))
        )
    ]
    parts = [
        copy(x_hbm.at[pl.ds(c * chunk, chunk)], x_ref.at[pl.ds(c * chunk, chunk)], 4 + c) for c in range(CHUNKS)
    ]
    tables = [copy(s_hbm, s_ref, 4 + CHUNKS), copy(f_hbm, f_ref, 5 + CHUNKS)]
    for made in small:
        made.wait()
    core = lax.axis_index("img") % 2
    coefficients = [float(v) for v in sine_coefficients()]
    wide_ref[...] = jnp.broadcast_to(focus_ref[...].astype(f32), (LANES, number)).T
    spread = spread_matrix(pose_ref[...], label_ref[...], planes, 0)
    spread_ref[...] = spread
    turns = turns_ref[...]

    def weigh(i, carry):
        angle = turns * wide_ref[pl.ds(i, 1), :] + 0.1 / (2 * math.pi)
        f = angle - jnp.round(angle)
        square = f * f
        poly = jnp.full(f.shape, coefficients[-1], f32)
        for coefficient in coefficients[-2::-1]:
            poly = poly * square + coefficient
        ctf = poly * f
        at = pl.multiple_of(i * 2 * ROWS, 2 * ROWS)
        rows = x_ref[pl.ds(at, 2 * ROWS), :].astype(f32)
        w_ref[pl.ds(at, ROWS), :] = ctf * rows[:ROWS]
        w_ref[pl.ds(at + ROWS, ROWS), :] = ctf * rows[ROWS:]
        return carry

    for c in range(CHUNKS):
        parts[c].wait()
        lax.fori_loop(c * number // CHUNKS, (c + 1) * number // CHUNKS, weigh, 0, unroll=UNROLL)

    def gather(r, ky):
        columns = [
            w_ref[pl.ds(r * ROWS + j * KY + ky, number, stride=2 * ROWS), :] for j in range(QUARTERS)
        ]
        return jnp.concatenate(columns, axis=1).astype(bf16)

    for r in range(2):
        for y in range(2):
            rows_ref[r, y] = gather(r, 2 * y + core)
    for made in tables:
        made.wait()
    transform(
        lambda r, y: gather(r, 2 * y + 1 - core),
        spread,
        lambda: s_ref[...],
        lambda p: f_ref[p * 2 * LANES : (p + 1) * 2 * LANES, :],
        v_ref,
        place(out_ref),
    )


def second_kernel(rows_ref, spread_ref, s_ref, f_ref, out_ref, v_ref):
    transform(
        lambda r, y: rows_ref[r, y],
        spread_ref[...],
        lambda: s_ref[...],
        lambda p: f_ref[p * 2 * LANES : (p + 1) * 2 * LANES, :],
        v_ref,
        place(out_ref),
    )


def last_kernel(scale, kept_ref, *refs):
    *got_refs, table_ref, out_ref = refs
    total = kept_ref[...].astype(f32)
    for got_ref in got_refs:
        total += got_ref[...].astype(f32)
    total = total.astype(bf16)
    turned = jnp.dot(table_ref[0], total[:, :LANES], preferred_element_type=f32)
    turned += jnp.dot(table_ref[1], total[:, LANES:], preferred_element_type=f32)
    out_ref[...] = turned * scale


def z_table(planes):
    z = np.arange(planes)
    angle = 2.0 * np.pi * ((z[:, None] * z[None, :]) % planes) / planes
    cos, sin = np.cos(angle), np.sin(angle)
    return np.stack([np.concatenate([cos, sin]), np.concatenate([-sin, cos])]).astype(jnp.bfloat16)


VMEM = pl.BlockSpec(memory_space=pltpu.VMEM)
SMEM = pl.BlockSpec(memory_space=pltpu.SMEM)
HBM = pl.BlockSpec(memory_space=pltpu.HBM)


def partner(axis, bit):
    return [(i, i ^ bit) for i in range(lax.axis_size(axis))]


def ctf_weights(defocus):
    x_index = jnp.arange(NX, dtype=jnp.int32)
    signed = (x_index + NX // 2) % NX - NX // 2
    y_index = jnp.arange(KY, dtype=jnp.int32) + 1
    radius = (y_index[:, None] ** 2 + signed[None, :] ** 2).astype(f32) / float(NX * NX)
    phase = 400.0 * math.pi * defocus.astype(f32)[:, None, None] * radius[None]
    return jnp.sin(phase + 0.1)


def many_planes(images, pose_bins, labels, defocus):
    owners, groups = lax.axis_size("slab"), lax.axis_size("img")
    number = images.shape[0]
    planes = owners * 4
    weighted = (ctf_weights(defocus)[:, None] * images.astype(f32)).astype(bf16)
    table_s = jnp.asarray(shift_table()).reshape(XBINS, NX, NX)
    table_f = jnp.asarray(fourier_table()).reshape(QUARTERS, 2, LANES, 2, LANES)

    def block(first_plane):
        spread = spread_matrix(pose_bins[None], labels[None], planes, first_plane)
        part = jnp.einsum("mi,irkx->rkmx", spread, weighted, preferred_element_type=f32).astype(bf16)
        part = part.reshape(2, KY, XBINS, CLASSES * PLANES, NX)
        placed = jnp.einsum("rkbcx,bxw->rkcw", part, table_s, preferred_element_type=f32).astype(bf16)
        placed = placed.reshape(2, KY, CLASSES, PLANES, QUARTERS, LANES)
        g0, g1, g2, g3 = jnp.einsum("rkczpm,prmsn->pkcnsz", placed, table_f, preferred_element_type=f32)
        a, b, c, d = g0 + g2, g0 - g2, g1 + g3, g1 - g3
        turned = jnp.stack([-d[..., 1, :], d[..., 0, :]], axis=-2)
        return jnp.stack([a + c, b + turned, a - c, b - turned], axis=2).astype(bf16)

    parts = lax.map(block, jnp.arange(planes // PLANES, dtype=jnp.int32) * PLANES)
    parts = jnp.moveaxis(parts, 0, -2).reshape(KY, CLASSES * NX, 2, planes).astype(f32)
    total = lax.psum_scatter(parts, "img", scatter_dimension=0, tiled=True)
    total = lax.psum_scatter(total, "slab", scatter_dimension=1, tiled=True)
    table = jnp.asarray(z_table(planes).astype(np.float32)).reshape(2, 2, planes, planes)
    scale = 2.5 / math.sqrt(number * owners * groups * NX)
    return scale * jnp.einsum("yqsz,stwz->yqtw", total, table, precision=lax.Precision.HIGHEST)


def on_device(images, pose_bins, labels, defocus):
    owners, groups = lax.axis_size("slab"), lax.axis_size("img")
    number = images.shape[0]
    planes = owners * 4
    if planes != PLANES:
        return many_planes(images, pose_bins, labels, defocus)
    scale = 2.5 / math.sqrt(number * owners * groups * NX)
    x = images.reshape(number, 2, KY, QUARTERS, LANES).transpose(0, 1, 3, 2, 4).reshape(number * 2 * ROWS, LANES)
    pieces = 2 * CLASSES * QUARTERS
    rows_shape = jax.ShapeDtypeStruct((2, 2, number, NX), bf16)
    spread_shape = jax.ShapeDtypeStruct((XBINS * CLASSES * PLANES, number), bf16)
    piece_shape = jax.ShapeDtypeStruct((pieces, PLANES, 2 * LANES), bf16)
    v_scratch = pltpu.VMEM((2 * 2 * CLASSES * PLANES, XBINS * NX), bf16)
    table_s, table_f = jnp.asarray(shift_table()), jnp.asarray(fourier_table())
    table_shapes = [jax.ShapeDtypeStruct(t.shape, bf16) for t in (table_s, table_f)]
    other, rows, spread, near_s, near_f = pl.pallas_call(
        functools.partial(first_kernel, planes),
        out_shape=(piece_shape, rows_shape, spread_shape, *table_shapes),
        in_specs=[HBM] * 7,
        out_specs=(VMEM,) * 5,
        scratch_shapes=[
            pltpu.VMEM(x.shape, bf16),
            pltpu.VMEM((1, number), bf16),
            pltpu.VMEM((1, number), jnp.int32),
            pltpu.VMEM((1, number), jnp.int32),
            pltpu.VMEM((ROWS, LANES), f32),
            pltpu.VMEM((number, LANES), f32),
            pltpu.VMEM(x.shape, f32),
            v_scratch,
            pltpu.SemaphoreType.DMA((CHUNKS + 6,)),
        ],
        compiler_params=pltpu.CompilerParams(vmem_limit_bytes=32 << 20),
        name="weigh_and_transform_other",
    )(*(
        pltpu.with_memory_space_constraint(v, pltpu.HBM)
        for v in (x, defocus[None], pose_bins[None], labels[None], jnp.asarray(turns_per_defocus()), table_s, table_f)
    ))
    got = lax.ppermute(other, "img", partner("img", 1))
    own = pl.pallas_call(
        second_kernel,
        out_shape=piece_shape,
        in_specs=[VMEM] * 4,
        out_specs=VMEM,
        scratch_shapes=[v_scratch],
        compiler_params=pltpu.CompilerParams(vmem_limit_bytes=16 << 20),
        name="transform_own",
    )(rows, spread, near_s, near_f)
    total = (own.astype(f32) + got.astype(f32)).astype(bf16)
    pieces = [total[3 * 4 : 4 * 4], total[2 * 4 : 3 * 4], total[4 : 2 * 4]]
    flat = owners * groups
    got = [
        lax.ppermute(piece, ("slab", "img"), [(i, i ^ flip) for i in range(flat)])
        for piece, flip in zip(pieces, (6, 4, 2))
    ]
    total = sum((g.astype(f32) for g in got), total[:4].astype(f32)).astype(bf16)
    pieces = [total[3], total[2], total[1]]
    got = [
        lax.ppermute(piece, ("slab", "img"), [(i, i ^ flip) for i in range(flat)])
        for piece, flip in zip(pieces, (24, 16, 8))
    ]
    out = pl.pallas_call(
        functools.partial(last_kernel, scale),
        out_shape=jax.ShapeDtypeStruct((2 * planes, LANES), f32),
        in_specs=[VMEM] * 5,
        out_specs=VMEM,
        compiler_params=pltpu.CompilerParams(vmem_limit_bytes=16 << 20),
        name="transform_planes",
    )(total[0], *got, jnp.asarray(z_table(planes)))
    return out.reshape(1, 2, planes, LANES).transpose(0, 3, 1, 2)


def solution(mesh):
    placed = (
        P(("slab", "img"), None, None, None),
        P(("slab", "img")),
        P(("slab", "img")),
        P(("slab", "img")),
    )
    return jax.shard_map(
        on_device, mesh=mesh, in_specs=placed, out_specs=P("img", "slab", None, None), check_vma=False
    )
```

```python
import functools
import math

import jax
import jax.numpy as jnp
import numpy as np
from jax import lax
from jax.experimental import pallas as pl
from jax.experimental.pallas import tpu as pltpu
from jax.sharding import PartitionSpec as P

NX = 512
KY = 4
CLASSES = 2
ZBINS = 4
XBINS = 4
TAPS = 8
LANES = 128
QUARTERS = NX // LANES
GROUP = LANES // QUARTERS
PLANES = 32
CHUNKS = 4
UNROLL = 8
ROWS = QUARTERS * KY
bf16, f32 = jnp.bfloat16, jnp.float32


def lanczos_taps(num_bins):
    fraction = (np.arange(num_bins, dtype=np.float32) + np.float32(0.5)) / np.float32(num_bins)
    distance = (np.arange(TAPS, dtype=np.float32) - np.float32(3.0))[None, :] - fraction[:, None]
    kernel = (np.sinc(distance) * np.sinc(distance / np.float32(4.0))).astype(np.float32)
    return (kernel / kernel.sum(-1, keepdims=True)).astype(jnp.bfloat16).astype(np.float32)


def turns_per_defocus():
    x = np.arange(NX)
    signed = (x + NX // 2) % NX - NX // 2
    y = np.arange(KY) + 1
    radius = 200.0 * (y[:, None] ** 2 + signed[None, :] ** 2) / NX**2
    table = radius.reshape(KY, QUARTERS, LANES).transpose(1, 0, 2).reshape(ROWS, LANES)
    return table.astype(np.float32)


def fourier_table():
    taps = lanczos_taps(XBINS).astype(np.float64)
    m = np.arange(LANES)
    group, lane = np.arange(LANES) // GROUP, np.arange(LANES) % GROUP
    out = np.zeros((QUARTERS, XBINS, LANES, 2, LANES))
    for q in range(QUARTERS):
        column = 4 * (GROUP * ((group - q) % QUARTERS) + lane) + q
        shift = 2.0 * np.pi * (((np.arange(TAPS) - 3)[:, None] * column[None, :]) % NX) / NX
        wave = 2.0 * np.pi * ((m[:, None] * column[None, :]) % NX) / NX
        for b in range(XBINS):
            value = (taps[b][:, None] * np.exp(1j * shift)).sum(0)[None, :] * np.exp(1j * wave)
            out[q, b, :, 0], out[q, b, :, 1] = value.real, value.imag
    return out.reshape(QUARTERS, XBINS * LANES, 2 * LANES).astype(jnp.bfloat16)


def order_table():
    out = np.zeros((QUARTERS, LANES, LANES), np.float32)
    group, lane = np.arange(LANES) // GROUP, np.arange(LANES) % GROUP
    for quarter in range(QUARTERS):
        out[quarter, np.arange(LANES), 4 * lane + (group - quarter) % QUARTERS] = 1.0
    return out.astype(jnp.bfloat16)


def sine_coefficients(terms=5):
    f = 0.5 * np.cos(np.linspace(0.0, np.pi / 2, 4001))
    basis = f[:, None] ** (2 * np.arange(terms) + 1)
    return np.linalg.lstsq(basis, np.sin(2 * np.pi * f), rcond=None)[0].astype(np.float32)


def device_bits():
    slab, img = lax.axis_index("slab"), lax.axis_index("img")
    return img // 2, slab % 2, slab // 2 % 2, slab // 4


def quarter_sums(parts):
    (r0, i0), (r1, i1), (r2, i2), (r3, i3) = parts
    ar, ai, br, bi = r0 + r2, i0 + i2, r0 - r2, i0 - i2
    cr, ci, dr, di = r1 + r3, i1 + i3, r1 - r3, i1 - i3
    return (ar + cr, ai + ci), (br - di, bi + dr), (ar - cr, ai - ci), (br + di, bi - dr)


def transform(w_ref, ky_low, spread, table, u_ref, v_ref, put):
    cz = CLASSES * PLANES
    number = spread.shape[1]
    for y in range(2):

        def column(r, p):
            return w_ref[pl.ds(r * ROWS + p * KY + 2 * y + ky_low, number, stride=2 * ROWS), :]

        sums = quarter_sums([(column(0, p), column(1, p)) for p in range(QUARTERS)])
        for q in range(QUARTERS):
            for r in range(2):
                at = (r * QUARTERS + q) * LANES
                u_ref[y, :, at : at + LANES] = sums[q][r].astype(bf16)
    for y in range(2):
        part = jnp.dot(spread, u_ref[y], preferred_element_type=f32).astype(bf16)
        for r in range(2):
            for q in range(QUARTERS):
                at, row = (r * QUARTERS + q) * LANES, (r * 2 + y) * cz
                for b in range(XBINS):
                    v_ref[q, row : row + cz, b * LANES : (b + 1) * LANES] = part[b * cz : (b + 1) * cz, at : at + LANES]
    group = lax.broadcasted_iota(jnp.int32, (2 * cz, LANES), 1) // GROUP
    real, imag = [], []
    for q in range(QUARTERS):
        both = jnp.dot(v_ref[q], table(q), preferred_element_type=f32)
        real.append(both[: 2 * cz, :LANES] - both[2 * cz :, LANES:])
        imag.append(both[: 2 * cz, LANES:] + both[2 * cz :, :LANES])
    for quarter in range(QUARTERS):
        chosen = []
        for parts in (real, imag):
            value = parts[(0 - quarter) % QUARTERS]
            for j in range(1, QUARTERS):
                value = jnp.where(group == j, parts[(j - quarter) % QUARTERS], value)
            chosen.append(value.astype(bf16))
        value = jnp.concatenate(chosen, axis=1)
        for y in range(2):
            for cls in range(CLASSES):
                at = (y * CLASSES + cls) * PLANES
                put(y, cls, quarter, value[at : at + PLANES])


def spread_matrix(pose, label, planes, first_plane):
    per_pose = ZBINS * XBINS
    taps = lanczos_taps(ZBINS)
    start, zbin, xbin = pose // per_pose, pose // XBINS % ZBINS, pose % XBINS
    shape = (XBINS * CLASSES * PLANES, pose.shape[1])
    row = lax.broadcasted_iota(jnp.int32, shape, 0)
    tap = (first_plane + row % PLANES - start + planes) % planes
    tap = jnp.where(row // PLANES == xbin * CLASSES + label, tap, -1)
    out = jnp.zeros(shape, f32)
    for t in range(TAPS):
        weight = jnp.full(pose.shape, float(taps[0, t]), f32)
        for z in range(1, ZBINS):
            weight = jnp.where(zbin == z, float(taps[z, t]), weight)
        out = jnp.where(tap == t, weight, out)
    return out.astype(bf16)


def place(out_ref):
    my_y, my_x, my_z, my_class = device_bits()

    def put(y, cls, q, value):
        index = ((q % 2) ^ my_x) * 8 + (y ^ my_y) * 4 + (cls ^ my_class) * 2 + ((q // 2) ^ my_z)
        out_ref[index] = value

    return put


def first_kernel(planes, x_hbm, focus_hbm, pose_hbm, label_hbm, turns_hbm, table_hbm,
                 out_ref, w_ref, spread_ref, table_ref,
                 x_ref, focus_ref, pose_ref, label_ref, turns_ref, wide_ref, u_ref, v_ref, sems):
    number = wide_ref.shape[0]
    chunk = x_ref.shape[0] // CHUNKS

    def copy(source, target, at):
        made = pltpu.make_async_copy(source, target, sems.at[at])
        made.start()
        return made

    small = [
        copy(source, target, at)
        for at, (source, target) in enumerate(
            ((focus_hbm, focus_ref), (turns_hbm, turns_ref), (pose_hbm, pose_ref), (label_hbm, label_ref))
        )
    ]
    parts = [
        copy(x_hbm.at[pl.ds(c * chunk, chunk)], x_ref.at[pl.ds(c * chunk, chunk)], 4 + c) for c in range(CHUNKS)
    ]
    table = copy(table_hbm, table_ref, 4 + CHUNKS)
    for made in small:
        made.wait()
    core = lax.axis_index("img") % 2
    coefficients = [float(v) for v in sine_coefficients()]
    wide_ref[...] = jnp.broadcast_to(focus_ref[...].astype(f32), (LANES, number)).T
    spread_ref[...] = spread_matrix(pose_ref[...], label_ref[...], planes, 0)
    turns = turns_ref[...]

    def weigh(i, carry):
        angle = turns * wide_ref[pl.ds(i, 1), :] + 0.1 / (2 * math.pi)
        f = angle - jnp.round(angle)
        square = f * f
        poly = jnp.full(f.shape, coefficients[-1], f32)
        for coefficient in coefficients[-2::-1]:
            poly = poly * square + coefficient
        ctf = poly * f
        at = pl.multiple_of(i * 2 * ROWS, 2 * ROWS)
        rows = x_ref[pl.ds(at, 2 * ROWS), :].astype(f32)
        w_ref[pl.ds(at, ROWS), :] = ctf * rows[:ROWS]
        w_ref[pl.ds(at + ROWS, ROWS), :] = ctf * rows[ROWS:]
        return carry

    for c in range(CHUNKS):
        parts[c].wait()
        lax.fori_loop(c * number // CHUNKS, (c + 1) * number // CHUNKS, weigh, 0, unroll=UNROLL)
    table.wait()
    transform(w_ref, 1 - core, spread_ref[...], lambda q: table_ref[q], u_ref, v_ref, place(out_ref))


def second_kernel(w_ref, spread_ref, table_ref, out_ref, u_ref, v_ref):
    core = lax.axis_index("img") % 2
    transform(w_ref, core, spread_ref[...], lambda q: table_ref[q], u_ref, v_ref, place(out_ref))


def last_kernel(scale, kept_ref, *refs):
    *got_refs, order_ref, table_ref, out_ref = refs
    total = kept_ref[...].astype(f32)
    for got_ref in got_refs:
        total += got_ref[...].astype(f32)
    total = total.astype(bf16)
    order = order_ref[lax.axis_index("slab") % QUARTERS]
    turned = 0.0
    for s in range(2):
        part = total[:, s * LANES : (s + 1) * LANES]
        part = jnp.dot(part, order, preferred_element_type=f32).astype(bf16)
        turned += jnp.dot(table_ref[s], part, preferred_element_type=f32)
    out_ref[...] = turned * scale


def z_table(planes):
    z = np.arange(planes)
    angle = 2.0 * np.pi * ((z[:, None] * z[None, :]) % planes) / planes
    cos, sin = np.cos(angle), np.sin(angle)
    return np.stack([np.concatenate([cos, sin]), np.concatenate([-sin, cos])]).astype(jnp.bfloat16)


VMEM = pl.BlockSpec(memory_space=pltpu.VMEM)
SMEM = pl.BlockSpec(memory_space=pltpu.SMEM)
HBM = pl.BlockSpec(memory_space=pltpu.HBM)


def partner(axis, bit):
    return [(i, i ^ bit) for i in range(lax.axis_size(axis))]


def ctf_weights(defocus):
    x_index = jnp.arange(NX, dtype=jnp.int32)
    signed = (x_index + NX // 2) % NX - NX // 2
    y_index = jnp.arange(KY, dtype=jnp.int32) + 1
    radius = (y_index[:, None] ** 2 + signed[None, :] ** 2).astype(f32) / float(NX * NX)
    phase = 400.0 * math.pi * defocus.astype(f32)[:, None, None] * radius[None]
    return jnp.sin(phase + 0.1)


def many_planes(images, pose_bins, labels, defocus):
    owners, groups = lax.axis_size("slab"), lax.axis_size("img")
    number = images.shape[0]
    planes = owners * 4
    weighted = (ctf_weights(defocus)[:, None] * images.astype(f32)).astype(bf16)
    table = jnp.asarray(fourier_table()).reshape(QUARTERS, XBINS, LANES, 2, LANES)
    order = jnp.asarray(order_table())
    quarters = jnp.moveaxis(weighted.astype(f32).reshape(number, 2, KY, QUARTERS, LANES), 3, 0)
    sums = quarter_sums([(part[:, 0], part[:, 1]) for part in quarters])
    sums = jnp.stack([jnp.stack(pair) for pair in sums]).astype(bf16)

    def block(first_plane):
        spread = spread_matrix(pose_bins[None], labels[None], planes, first_plane)
        spread = spread.reshape(XBINS, CLASSES * PLANES, number)
        part = jnp.einsum("bci,qrikm->qrkcbm", spread, sums, preferred_element_type=f32).astype(bf16)
        both = jnp.einsum("qrkcbm,qbmsn->rsqkcn", part, table, preferred_element_type=f32)
        turned = jnp.stack([both[0, 0] - both[1, 1], both[0, 1] + both[1, 0]])
        turned = turned.reshape(2, QUARTERS, KY, CLASSES, PLANES, QUARTERS, GROUP)
        ordered = []
        for quarter in range(QUARTERS):
            groups_of = [turned[:, (j - quarter) % QUARTERS, ..., j, :] for j in range(QUARTERS)]
            value = jnp.concatenate(groups_of, axis=-1).astype(bf16)
            ordered.append(jnp.einsum("skczn,nw->kcwsz", value, order[quarter], preferred_element_type=f32))
        return jnp.stack(ordered, axis=2).astype(bf16)

    parts = lax.map(block, jnp.arange(planes // PLANES, dtype=jnp.int32) * PLANES)
    parts = jnp.moveaxis(parts, 0, -2).reshape(KY, CLASSES * NX, 2, planes).astype(f32)
    total = lax.psum_scatter(parts, "img", scatter_dimension=0, tiled=True)
    total = lax.psum_scatter(total, "slab", scatter_dimension=1, tiled=True)
    table = jnp.asarray(z_table(planes).astype(np.float32)).reshape(2, 2, planes, planes)
    scale = 2.5 / math.sqrt(number * owners * groups * NX)
    return scale * jnp.einsum("yqsz,stwz->yqtw", total, table, precision=lax.Precision.HIGHEST)


def on_device(images, pose_bins, labels, defocus):
    owners, groups = lax.axis_size("slab"), lax.axis_size("img")
    number = images.shape[0]
    planes = owners * 4
    if planes != PLANES:
        return many_planes(images, pose_bins, labels, defocus)
    scale = 2.5 / math.sqrt(number * owners * groups * NX)
    x = images.reshape(number, 2, KY, QUARTERS, LANES).transpose(0, 1, 3, 2, 4).reshape(number * 2 * ROWS, LANES)
    pieces = 2 * CLASSES * QUARTERS
    w_shape = jax.ShapeDtypeStruct(x.shape, f32)
    spread_shape = jax.ShapeDtypeStruct((XBINS * CLASSES * PLANES, number), bf16)
    piece_shape = jax.ShapeDtypeStruct((pieces, PLANES, 2 * LANES), bf16)
    table = jnp.asarray(fourier_table())
    table_shape = jax.ShapeDtypeStruct(table.shape, bf16)
    work = [
        pltpu.VMEM((2, number, 2 * NX), bf16),
        pltpu.VMEM((QUARTERS, 4 * CLASSES * PLANES, XBINS * LANES), bf16),
    ]
    other, weighted, spread, near_table = pl.pallas_call(
        functools.partial(first_kernel, planes),
        out_shape=(piece_shape, w_shape, spread_shape, table_shape),
        in_specs=[HBM] * 6,
        out_specs=(VMEM,) * 4,
        scratch_shapes=[
            pltpu.VMEM(x.shape, bf16),
            pltpu.VMEM((1, number), bf16),
            pltpu.VMEM((1, number), jnp.int32),
            pltpu.VMEM((1, number), jnp.int32),
            pltpu.VMEM((ROWS, LANES), f32),
            pltpu.VMEM((number, LANES), f32),
            *work,
            pltpu.SemaphoreType.DMA((CHUNKS + 5,)),
        ],
        compiler_params=pltpu.CompilerParams(vmem_limit_bytes=32 << 20),
        name="weigh_and_transform_other",
    )(*(
        pltpu.with_memory_space_constraint(v, pltpu.HBM)
        for v in (x, defocus[None], pose_bins[None], labels[None], jnp.asarray(turns_per_defocus()), table)
    ))
    got = lax.ppermute(other, "img", partner("img", 1))
    own = pl.pallas_call(
        second_kernel,
        out_shape=piece_shape,
        in_specs=[VMEM] * 3,
        out_specs=VMEM,
        scratch_shapes=work,
        compiler_params=pltpu.CompilerParams(vmem_limit_bytes=16 << 20),
        name="transform_own",
    )(weighted, spread, near_table)
    total = (own.astype(f32) + got.astype(f32)).astype(bf16)
    pieces = [total[3 * 4 : 4 * 4], total[2 * 4 : 3 * 4], total[4 : 2 * 4]]
    flat = owners * groups
    got = [
        lax.ppermute(piece, ("slab", "img"), [(i, i ^ flip) for i in range(flat)])
        for piece, flip in zip(pieces, (6, 4, 2))
    ]
    total = sum((g.astype(f32) for g in got), total[:4].astype(f32)).astype(bf16)
    pieces = [total[1], total[3], total[2]]
    got = [
        lax.ppermute(piece, ("slab", "img"), [(i, i ^ flip) for i in range(flat)])
        for piece, flip in zip(pieces, (8, 24, 16))
    ]
    out = pl.pallas_call(
        functools.partial(last_kernel, scale),
        out_shape=jax.ShapeDtypeStruct((2 * planes, LANES), f32),
        in_specs=[VMEM] * 6,
        out_specs=VMEM,
        compiler_params=pltpu.CompilerParams(vmem_limit_bytes=16 << 20),
        name="transform_planes",
    )(total[0], *got, jnp.asarray(order_table()), jnp.asarray(z_table(planes)))
    return out.reshape(1, 2, planes, LANES).transpose(0, 3, 1, 2)


def solution(mesh):
    placed = (
        P(("slab", "img"), None, None, None),
        P(("slab", "img")),
        P(("slab", "img")),
        P(("slab", "img")),
    )
    return jax.shard_map(
        on_device, mesh=mesh, in_specs=placed, out_specs=P("img", "slab", None, None), check_vma=False
    )
```

```python
import functools
import math

import jax
import jax.numpy as jnp
import numpy as np
from jax import lax
from jax.experimental import pallas as pl
from jax.experimental.pallas import tpu as pltpu
from jax.sharding import PartitionSpec as P

NX = 512
KY = 4
CLASSES = 2
ZBINS = 4
XBINS = 4
TAPS = 8
LANES = 128
QUARTERS = NX // LANES
GROUP = LANES // QUARTERS
PLANES = 32
CHUNKS = 4
UNROLL = 8
ROWS = QUARTERS * KY
PITCH = 2 * ROWS + 1
bf16, f32 = jnp.bfloat16, jnp.float32


def lanczos_taps(num_bins):
    fraction = (np.arange(num_bins, dtype=np.float32) + np.float32(0.5)) / np.float32(num_bins)
    distance = (np.arange(TAPS, dtype=np.float32) - np.float32(3.0))[None, :] - fraction[:, None]
    kernel = (np.sinc(distance) * np.sinc(distance / np.float32(4.0))).astype(np.float32)
    return (kernel / kernel.sum(-1, keepdims=True)).astype(jnp.bfloat16).astype(np.float32)


def turns_per_defocus():
    x = np.arange(NX)
    signed = (x + NX // 2) % NX - NX // 2
    y = np.arange(KY) + 1
    radius = 200.0 * (y[:, None] ** 2 + signed[None, :] ** 2) / NX**2
    table = radius.reshape(KY, QUARTERS, LANES).transpose(1, 0, 2).reshape(ROWS, LANES)
    return table.astype(np.float32)


def fourier_table():
    taps = lanczos_taps(XBINS).astype(np.float64)
    m = np.arange(LANES)
    group, lane = np.arange(LANES) // GROUP, np.arange(LANES) % GROUP
    out = np.zeros((QUARTERS, XBINS, LANES, 2, LANES))
    for q in range(QUARTERS):
        column = 4 * (GROUP * ((group - q) % QUARTERS) + lane) + q
        shift = 2.0 * np.pi * (((np.arange(TAPS) - 3)[:, None] * column[None, :]) % NX) / NX
        wave = 2.0 * np.pi * ((m[:, None] * column[None, :]) % NX) / NX
        for b in range(XBINS):
            value = (taps[b][:, None] * np.exp(1j * shift)).sum(0)[None, :] * np.exp(1j * wave)
            out[q, b, :, 0], out[q, b, :, 1] = value.real, value.imag
    return out.reshape(QUARTERS, XBINS * LANES, 2 * LANES).astype(jnp.bfloat16)


def order_table():
    out = np.zeros((QUARTERS, LANES, LANES), np.float32)
    group, lane = np.arange(LANES) // GROUP, np.arange(LANES) % GROUP
    for quarter in range(QUARTERS):
        out[quarter, np.arange(LANES), 4 * lane + (group - quarter) % QUARTERS] = 1.0
    return out.astype(jnp.bfloat16)


def sine_coefficients(terms=5):
    f = 0.5 * np.cos(np.linspace(0.0, np.pi / 2, 4001))
    basis = f[:, None] ** (2 * np.arange(terms) + 1)
    return np.linalg.lstsq(basis, np.sin(2 * np.pi * f), rcond=None)[0].astype(np.float32)


def device_bits():
    slab, img = lax.axis_index("slab"), lax.axis_index("img")
    return img // 2, slab % 2, slab // 2 % 2, slab // 4


def quarter_sums(parts):
    (r0, i0), (r1, i1), (r2, i2), (r3, i3) = parts
    ar, ai, br, bi = r0 + r2, i0 + i2, r0 - r2, i0 - i2
    cr, ci, dr, di = r1 + r3, i1 + i3, r1 - r3, i1 - i3
    return (ar + cr, ai + ci), (br - di, bi + dr), (ar - cr, ai - ci), (br + di, bi - dr)


def transform(w_ref, ky_low, spread, table, u_ref, v_ref, put):
    cz = CLASSES * PLANES
    number = spread.shape[1]
    for y in range(2):

        def column(r, p):
            return w_ref[pl.ds(r * ROWS + p * KY + 2 * y + ky_low, number, stride=PITCH), :]

        sums = quarter_sums([(column(0, p), column(1, p)) for p in range(QUARTERS)])
        for q in range(QUARTERS):
            for r in range(2):
                at = (r * QUARTERS + q) * LANES
                u_ref[y, :, at : at + LANES] = sums[q][r].astype(bf16)
    for y in range(2):
        part = jnp.dot(spread, u_ref[y], preferred_element_type=f32).astype(bf16)
        for r in range(2):
            for q in range(QUARTERS):
                at, row = (r * QUARTERS + q) * LANES, (r * 2 + y) * cz
                for b in range(XBINS):
                    v_ref[q, row : row + cz, b * LANES : (b + 1) * LANES] = part[b * cz : (b + 1) * cz, at : at + LANES]
    group = lax.broadcasted_iota(jnp.int32, (2 * cz, LANES), 1) // GROUP
    real, imag = [], []
    for q in range(QUARTERS):
        both = jnp.dot(v_ref[q], table(q), preferred_element_type=f32)
        real.append(both[: 2 * cz, :LANES] - both[2 * cz :, LANES:])
        imag.append(both[: 2 * cz, LANES:] + both[2 * cz :, :LANES])
    for quarter in range(QUARTERS):
        chosen = []
        for parts in (real, imag):
            value = parts[(0 - quarter) % QUARTERS]
            for j in range(1, QUARTERS):
                value = jnp.where(group == j, parts[(j - quarter) % QUARTERS], value)
            chosen.append(value.astype(bf16))
        value = jnp.concatenate(chosen, axis=1)
        for y in range(2):
            for cls in range(CLASSES):
                at = (y * CLASSES + cls) * PLANES
                put(y, cls, quarter, value[at : at + PLANES])


def spread_matrix(pose, label, planes, first_plane):
    per_pose = ZBINS * XBINS
    taps = lanczos_taps(ZBINS)
    start, zbin, xbin = pose // per_pose, pose // XBINS % ZBINS, pose % XBINS
    shape = (XBINS * CLASSES * PLANES, pose.shape[1])
    row = lax.broadcasted_iota(jnp.int32, shape, 0)
    tap = (first_plane + row % PLANES - start + planes) % planes
    tap = jnp.where(row // PLANES == xbin * CLASSES + label, tap, -1)
    out = jnp.zeros(shape, f32)
    for t in range(TAPS):
        weight = jnp.full(pose.shape, float(taps[0, t]), f32)
        for z in range(1, ZBINS):
            weight = jnp.where(zbin == z, float(taps[z, t]), weight)
        out = jnp.where(tap == t, weight, out)
    return out.astype(bf16)


def place(out_ref):
    my_y, my_x, my_z, my_class = device_bits()

    def put(y, cls, q, value):
        index = ((q % 2) ^ my_x) * 8 + (y ^ my_y) * 4 + (cls ^ my_class) * 2 + ((q // 2) ^ my_z)
        out_ref[index] = value

    return put


def first_kernel(planes, x_hbm, focus_hbm, pose_hbm, label_hbm, turns_hbm, table_hbm,
                 out_ref, w_ref, spread_ref, table_ref,
                 x_ref, focus_ref, pose_ref, label_ref, turns_ref, wide_ref, u_ref, v_ref, sems):
    number = wide_ref.shape[0]
    chunk = x_ref.shape[0] // CHUNKS

    def copy(source, target, at):
        made = pltpu.make_async_copy(source, target, sems.at[at])
        made.start()
        return made

    small = [
        copy(source, target, at)
        for at, (source, target) in enumerate(
            ((focus_hbm, focus_ref), (turns_hbm, turns_ref), (pose_hbm, pose_ref), (label_hbm, label_ref))
        )
    ]
    parts = [
        copy(x_hbm.at[pl.ds(c * chunk, chunk)], x_ref.at[pl.ds(c * chunk, chunk)], 4 + c) for c in range(CHUNKS)
    ]
    table = copy(table_hbm, table_ref, 4 + CHUNKS)
    for made in small:
        made.wait()
    core = lax.axis_index("img") % 2
    coefficients = [float(v) for v in sine_coefficients()]
    wide_ref[...] = jnp.broadcast_to(focus_ref[...].astype(f32), (LANES, number)).T
    spread_ref[...] = spread_matrix(pose_ref[...], label_ref[...], planes, 0)
    turns = turns_ref[...]

    def weigh(i, carry):
        angle = turns * wide_ref[pl.ds(i, 1), :] + 0.1 / (2 * math.pi)
        f = angle - jnp.round(angle)
        square = f * f
        poly = jnp.full(f.shape, coefficients[-1], f32)
        for coefficient in coefficients[-2::-1]:
            poly = poly * square + coefficient
        ctf = poly * f
        at = pl.multiple_of(i * 2 * ROWS, 2 * ROWS)
        rows = x_ref[pl.ds(at, 2 * ROWS), :].astype(f32)
        w_ref[pl.ds(i * PITCH, ROWS), :] = ctf * rows[:ROWS]
        w_ref[pl.ds(i * PITCH + ROWS, ROWS), :] = ctf * rows[ROWS:]
        return carry

    for c in range(CHUNKS):
        parts[c].wait()
        lax.fori_loop(c * number // CHUNKS, (c + 1) * number // CHUNKS, weigh, 0, unroll=UNROLL)
    table.wait()
    transform(w_ref, 1 - core, spread_ref[...], lambda q: table_ref[q], u_ref, v_ref, place(out_ref))


def second_kernel(w_ref, spread_ref, table_ref, out_ref, u_ref, v_ref):
    core = lax.axis_index("img") % 2
    transform(w_ref, core, spread_ref[...], lambda q: table_ref[q], u_ref, v_ref, place(out_ref))


def last_kernel(scale, *refs):
    *got_refs, order_ref, table_ref, out_ref = refs
    total = sum(got_ref[...].astype(f32) for got_ref in got_refs)
    total = total.astype(bf16)
    order = order_ref[lax.axis_index("slab") % QUARTERS]
    turned = 0.0
    for s in range(2):
        part = total[:, s * LANES : (s + 1) * LANES]
        part = jnp.dot(part, order, preferred_element_type=f32).astype(bf16)
        turned += jnp.dot(table_ref[s], part, preferred_element_type=f32)
    out_ref[...] = turned * scale


def z_table(planes):
    z = np.arange(planes)
    angle = 2.0 * np.pi * ((z[:, None] * z[None, :]) % planes) / planes
    cos, sin = np.cos(angle), np.sin(angle)
    return np.stack([np.concatenate([cos, sin]), np.concatenate([-sin, cos])]).astype(jnp.bfloat16)


VMEM = pl.BlockSpec(memory_space=pltpu.VMEM)
SMEM = pl.BlockSpec(memory_space=pltpu.SMEM)
HBM = pl.BlockSpec(memory_space=pltpu.HBM)


FIRST = (1, 1 + 2, 1 + 4, 1 + 2 + 4)
SECOND = (1, 1 + 8, 1 + 16, 1 + 8 + 16)
FIRST_ORDER = (3, 2, 1, 0)
SECOND_ORDER = (0, 1, 3, 2)


def passed(piece, flip):
    flat = lax.axis_size("slab") * lax.axis_size("img")
    return lax.ppermute(piece, ("slab", "img"), [(i, i ^ flip) for i in range(flat)])


def ctf_weights(defocus):
    x_index = jnp.arange(NX, dtype=jnp.int32)
    signed = (x_index + NX // 2) % NX - NX // 2
    y_index = jnp.arange(KY, dtype=jnp.int32) + 1
    radius = (y_index[:, None] ** 2 + signed[None, :] ** 2).astype(f32) / float(NX * NX)
    phase = 400.0 * math.pi * defocus.astype(f32)[:, None, None] * radius[None]
    return jnp.sin(phase + 0.1)


def many_planes(images, pose_bins, labels, defocus):
    owners, groups = lax.axis_size("slab"), lax.axis_size("img")
    number = images.shape[0]
    planes = owners * 4
    weighted = (ctf_weights(defocus)[:, None] * images.astype(f32)).astype(bf16)
    table = jnp.asarray(fourier_table()).reshape(QUARTERS, XBINS, LANES, 2, LANES)
    order = jnp.asarray(order_table())
    quarters = jnp.moveaxis(weighted.astype(f32).reshape(number, 2, KY, QUARTERS, LANES), 3, 0)
    sums = quarter_sums([(part[:, 0], part[:, 1]) for part in quarters])
    sums = jnp.stack([jnp.stack(pair) for pair in sums]).astype(bf16)

    def block(first_plane):
        spread = spread_matrix(pose_bins[None], labels[None], planes, first_plane)
        spread = spread.reshape(XBINS, CLASSES * PLANES, number)
        part = jnp.einsum("bci,qrikm->qrkcbm", spread, sums, preferred_element_type=f32).astype(bf16)
        both = jnp.einsum("qrkcbm,qbmsn->rsqkcn", part, table, preferred_element_type=f32)
        turned = jnp.stack([both[0, 0] - both[1, 1], both[0, 1] + both[1, 0]])
        turned = turned.reshape(2, QUARTERS, KY, CLASSES, PLANES, QUARTERS, GROUP)
        ordered = []
        for quarter in range(QUARTERS):
            groups_of = [turned[:, (j - quarter) % QUARTERS, ..., j, :] for j in range(QUARTERS)]
            value = jnp.concatenate(groups_of, axis=-1).astype(bf16)
            ordered.append(jnp.einsum("skczn,nw->kcwsz", value, order[quarter], preferred_element_type=f32))
        return jnp.stack(ordered, axis=2).astype(bf16)

    parts = lax.map(block, jnp.arange(planes // PLANES, dtype=jnp.int32) * PLANES)
    parts = jnp.moveaxis(parts, 0, -2).reshape(KY, CLASSES * NX, 2, planes).astype(f32)
    total = lax.psum_scatter(parts, "img", scatter_dimension=0, tiled=True)
    total = lax.psum_scatter(total, "slab", scatter_dimension=1, tiled=True)
    table = jnp.asarray(z_table(planes).astype(np.float32)).reshape(2, 2, planes, planes)
    scale = 2.5 / math.sqrt(number * owners * groups * NX)
    return scale * jnp.einsum("yqsz,stwz->yqtw", total, table, precision=lax.Precision.HIGHEST)


def on_device(images, pose_bins, labels, defocus):
    owners, groups = lax.axis_size("slab"), lax.axis_size("img")
    number = images.shape[0]
    planes = owners * 4
    if planes != PLANES:
        return many_planes(images, pose_bins, labels, defocus)
    scale = 2.5 / math.sqrt(number * owners * groups * NX)
    x = images.reshape(number, 2, KY, QUARTERS, LANES).transpose(0, 1, 3, 2, 4).reshape(number * 2 * ROWS, LANES)
    pieces = 2 * CLASSES * QUARTERS
    w_shape = jax.ShapeDtypeStruct((number * PITCH, LANES), f32)
    spread_shape = jax.ShapeDtypeStruct((XBINS * CLASSES * PLANES, number), bf16)
    piece_shape = jax.ShapeDtypeStruct((pieces, PLANES, 2 * LANES), bf16)
    table = jnp.asarray(fourier_table())
    table_shape = jax.ShapeDtypeStruct(table.shape, bf16)
    work = [
        pltpu.VMEM((2, number, 2 * NX), bf16),
        pltpu.VMEM((QUARTERS, 4 * CLASSES * PLANES, XBINS * LANES), bf16),
    ]
    other, weighted, spread, near_table = pl.pallas_call(
        functools.partial(first_kernel, planes),
        out_shape=(piece_shape, w_shape, spread_shape, table_shape),
        in_specs=[HBM] * 6,
        out_specs=(VMEM,) * 4,
        scratch_shapes=[
            pltpu.VMEM(x.shape, bf16),
            pltpu.VMEM((1, number), bf16),
            pltpu.VMEM((1, number), jnp.int32),
            pltpu.VMEM((1, number), jnp.int32),
            pltpu.VMEM((ROWS, LANES), f32),
            pltpu.VMEM((number, LANES), f32),
            *work,
            pltpu.SemaphoreType.DMA((CHUNKS + 5,)),
        ],
        compiler_params=pltpu.CompilerParams(vmem_limit_bytes=32 << 20),
        name="weigh_and_transform_other",
    )(*(
        pltpu.with_memory_space_constraint(v, pltpu.HBM)
        for v in (x, defocus[None], pose_bins[None], labels[None], jnp.asarray(turns_per_defocus()), table)
    ))
    got = passed(other, 1)
    own = pl.pallas_call(
        second_kernel,
        out_shape=piece_shape,
        in_specs=[VMEM] * 3,
        out_specs=VMEM,
        scratch_shapes=work,
        compiler_params=pltpu.CompilerParams(vmem_limit_bytes=16 << 20),
        name="transform_own",
    )(weighted, spread, near_table)
    total = (own.astype(f32) + got.astype(f32)).astype(bf16)
    got = [passed(total[4 * group : 4 * group + 4], FIRST[group]) for group in FIRST_ORDER]
    total = sum(g.astype(f32) for g in got).astype(bf16)
    got = [passed(total[group], SECOND[group]) for group in SECOND_ORDER]
    out = pl.pallas_call(
        functools.partial(last_kernel, scale),
        out_shape=jax.ShapeDtypeStruct((2 * planes, LANES), f32),
        in_specs=[VMEM] * 6,
        out_specs=VMEM,
        compiler_params=pltpu.CompilerParams(vmem_limit_bytes=16 << 20),
        name="transform_planes",
    )(*got, jnp.asarray(order_table()), jnp.asarray(z_table(planes)))
    return out.reshape(1, 2, planes, LANES).transpose(0, 3, 1, 2)


def solution(mesh):
    placed = (
        P(("slab", "img"), None, None, None),
        P(("slab", "img")),
        P(("slab", "img")),
        P(("slab", "img")),
    )
    return jax.shard_map(
        on_device, mesh=mesh, in_specs=placed, out_specs=P("img", "slab", None, None), check_vma=False
    )
```

```python
import functools
import math

import jax
import jax.numpy as jnp
import numpy as np
from jax import lax
from jax.experimental import pallas as pl
from jax.experimental.pallas import tpu as pltpu
from jax.sharding import PartitionSpec as P

NX = 512
KY = 4
CLASSES = 2
ZBINS = 4
XBINS = 4
TAPS = 8
LANES = 128
QUARTERS = NX // LANES
GROUP = LANES // QUARTERS
PLANES = 32
CHUNKS = 4
UNROLL = 8
ROWS = QUARTERS * KY
PITCH = 2 * ROWS + 1
bf16, f32 = jnp.bfloat16, jnp.float32


def lanczos_taps(num_bins):
    fraction = (np.arange(num_bins, dtype=np.float32) + np.float32(0.5)) / np.float32(num_bins)
    distance = (np.arange(TAPS, dtype=np.float32) - np.float32(3.0))[None, :] - fraction[:, None]
    kernel = (np.sinc(distance) * np.sinc(distance / np.float32(4.0))).astype(np.float32)
    return (kernel / kernel.sum(-1, keepdims=True)).astype(jnp.bfloat16).astype(np.float32)


def turns_per_defocus():
    x = np.arange(NX)
    signed = (x + NX // 2) % NX - NX // 2
    y = np.arange(KY) + 1
    radius = 200.0 * (y[:, None] ** 2 + signed[None, :] ** 2) / NX**2
    table = radius.reshape(KY, QUARTERS, LANES).transpose(1, 0, 2).reshape(ROWS, LANES)
    return table.astype(np.float32)


def fourier_table():
    taps = lanczos_taps(XBINS).astype(np.float64)
    m = np.arange(LANES)
    group, lane = np.arange(LANES) // GROUP, np.arange(LANES) % GROUP
    out = np.zeros((QUARTERS, XBINS, LANES, 2, LANES))
    for q in range(QUARTERS):
        column = 4 * (GROUP * ((group - q) % QUARTERS) + lane) + q
        shift = 2.0 * np.pi * (((np.arange(TAPS) - 3)[:, None] * column[None, :]) % NX) / NX
        wave = 2.0 * np.pi * ((m[:, None] * column[None, :]) % NX) / NX
        for b in range(XBINS):
            value = (taps[b][:, None] * np.exp(1j * shift)).sum(0)[None, :] * np.exp(1j * wave)
            out[q, b, :, 0], out[q, b, :, 1] = value.real, value.imag
    return out.reshape(QUARTERS, XBINS * LANES, 2 * LANES).astype(jnp.bfloat16)


def order_table():
    out = np.zeros((QUARTERS, LANES, LANES), np.float32)
    group, lane = np.arange(LANES) // GROUP, np.arange(LANES) % GROUP
    for quarter in range(QUARTERS):
        out[quarter, np.arange(LANES), 4 * lane + (group - quarter) % QUARTERS] = 1.0
    return out.astype(jnp.bfloat16)


def sine_coefficients(terms=5):
    f = 0.5 * np.cos(np.linspace(0.0, np.pi / 2, 4001))
    basis = f[:, None] ** (2 * np.arange(terms) + 1)
    return np.linalg.lstsq(basis, np.sin(2 * np.pi * f), rcond=None)[0].astype(np.float32)


def slot_of(schedule, here, there):
    slots = [[row[at] for row in schedule].index(there) for at in range(4)]
    slot = jnp.int32(slots[0])
    for at in range(1, 4):
        slot = jnp.where(here == at, slots[at], slot)
    return slot


def quarter_sums(parts):
    (r0, i0), (r1, i1), (r2, i2), (r3, i3) = parts
    ar, ai, br, bi = r0 + r2, i0 + i2, r0 - r2, i0 - i2
    cr, ci, dr, di = r1 + r3, i1 + i3, r1 - r3, i1 - i3
    return (ar + cr, ai + ci), (br - di, bi + dr), (ar - cr, ai - ci), (br + di, bi - dr)


def transform(w_ref, ky_low, spread, table, u_ref, v_ref, put):
    cz = CLASSES * PLANES
    number = spread.shape[1]
    for y in range(2):

        def column(r, p):
            return w_ref[pl.ds(r * ROWS + p * KY + 2 * y + ky_low, number, stride=PITCH), :]

        sums = quarter_sums([(column(0, p), column(1, p)) for p in range(QUARTERS)])
        for q in range(QUARTERS):
            for r in range(2):
                at = (r * QUARTERS + q) * LANES
                u_ref[y, :, at : at + LANES] = sums[q][r].astype(bf16)
    for y in range(2):
        part = jnp.dot(spread, u_ref[y], preferred_element_type=f32).astype(bf16)
        for r in range(2):
            for q in range(QUARTERS):
                at, row = (r * QUARTERS + q) * LANES, (r * 2 + y) * cz
                for b in range(XBINS):
                    v_ref[q, row : row + cz, b * LANES : (b + 1) * LANES] = part[b * cz : (b + 1) * cz, at : at + LANES]
    group = lax.broadcasted_iota(jnp.int32, (2 * cz, LANES), 1) // GROUP
    real, imag = [], []
    for q in range(QUARTERS):
        both = jnp.dot(v_ref[q], table(q), preferred_element_type=f32)
        real.append(both[: 2 * cz, :LANES] - both[2 * cz :, LANES:])
        imag.append(both[: 2 * cz, LANES:] + both[2 * cz :, :LANES])
    for quarter in range(QUARTERS):
        chosen = []
        for parts in (real, imag):
            value = parts[(0 - quarter) % QUARTERS]
            for j in range(1, QUARTERS):
                value = jnp.where(group == j, parts[(j - quarter) % QUARTERS], value)
            chosen.append(value.astype(bf16))
        value = jnp.concatenate(chosen, axis=1)
        for y in range(2):
            for cls in range(CLASSES):
                at = (y * CLASSES + cls) * PLANES
                put(y, cls, quarter, value[at : at + PLANES])


def spread_matrix(pose, label, planes, first_plane):
    per_pose = ZBINS * XBINS
    taps = lanczos_taps(ZBINS)
    start, zbin, xbin = pose // per_pose, pose // XBINS % ZBINS, pose % XBINS
    shape = (XBINS * CLASSES * PLANES, pose.shape[1])
    row = lax.broadcasted_iota(jnp.int32, shape, 0)
    tap = (first_plane + row % PLANES - start + planes) % planes
    tap = jnp.where(row // PLANES == xbin * CLASSES + label, tap, -1)
    out = jnp.zeros(shape, f32)
    for t in range(TAPS):
        weight = jnp.full(pose.shape, float(taps[0, t]), f32)
        for z in range(1, ZBINS):
            weight = jnp.where(zbin == z, float(taps[z, t]), weight)
        out = jnp.where(tap == t, weight, out)
    return out.astype(bf16)


def place(out_ref):
    slab, img = lax.axis_index("slab"), lax.axis_index("img")
    here = slab % 2 * 2 + img // 2
    first = [slot_of(FIRST, here, there) for there in range(4)]
    second = [slot_of(SECOND, slab // 2, there) for there in range(4)]

    def put(y, cls, quarter, value):
        out_ref[first[quarter % 2 * 2 + y] * 4 + second[cls * 2 + quarter // 2]] = value

    return put


def first_kernel(planes, x_hbm, focus_hbm, pose_hbm, label_hbm, turns_hbm, table_hbm,
                 out_ref, w_ref, spread_ref, table_ref,
                 x_ref, focus_ref, pose_ref, label_ref, turns_ref, wide_ref, u_ref, v_ref, sems):
    number = wide_ref.shape[0]
    chunk = x_ref.shape[0] // CHUNKS

    def copy(source, target, at):
        made = pltpu.make_async_copy(source, target, sems.at[at])
        made.start()
        return made

    small = [
        copy(source, target, at)
        for at, (source, target) in enumerate(
            ((focus_hbm, focus_ref), (turns_hbm, turns_ref), (pose_hbm, pose_ref), (label_hbm, label_ref))
        )
    ]
    parts = [
        copy(x_hbm.at[pl.ds(c * chunk, chunk)], x_ref.at[pl.ds(c * chunk, chunk)], 4 + c) for c in range(CHUNKS)
    ]
    table = copy(table_hbm, table_ref, 4 + CHUNKS)
    for made in small:
        made.wait()
    core = lax.axis_index("img") % 2
    coefficients = [float(v) for v in sine_coefficients()]
    wide_ref[...] = jnp.broadcast_to(focus_ref[...].astype(f32), (LANES, number)).T
    spread_ref[...] = spread_matrix(pose_ref[...], label_ref[...], planes, 0)
    turns = turns_ref[...]

    def weigh(i, carry):
        angle = turns * wide_ref[pl.ds(i, 1), :] + 0.1 / (2 * math.pi)
        f = angle - jnp.round(angle)
        square = f * f
        poly = jnp.full(f.shape, coefficients[-1], f32)
        for coefficient in coefficients[-2::-1]:
            poly = poly * square + coefficient
        ctf = poly * f
        at = pl.multiple_of(i * 2 * ROWS, 2 * ROWS)
        rows = x_ref[pl.ds(at, 2 * ROWS), :].astype(f32)
        w_ref[pl.ds(i * PITCH, ROWS), :] = ctf * rows[:ROWS]
        w_ref[pl.ds(i * PITCH + ROWS, ROWS), :] = ctf * rows[ROWS:]
        return carry

    for c in range(CHUNKS):
        parts[c].wait()
        lax.fori_loop(c * number // CHUNKS, (c + 1) * number // CHUNKS, weigh, 0, unroll=UNROLL)
    table.wait()
    transform(w_ref, 1 - core, spread_ref[...], lambda q: table_ref[q], u_ref, v_ref, place(out_ref))


def second_kernel(w_ref, spread_ref, table_ref, out_ref, u_ref, v_ref):
    core = lax.axis_index("img") % 2
    transform(w_ref, core, spread_ref[...], lambda q: table_ref[q], u_ref, v_ref, place(out_ref))


def last_kernel(scale, *refs):
    *got_refs, order_ref, table_ref, out_ref = refs
    total = sum(got_ref[...].astype(f32) for got_ref in got_refs)
    total = total.astype(bf16)
    order = order_ref[lax.axis_index("slab") % QUARTERS]
    turned = 0.0
    for s in range(2):
        part = total[:, s * LANES : (s + 1) * LANES]
        part = jnp.dot(part, order, preferred_element_type=f32).astype(bf16)
        turned += jnp.dot(table_ref[s], part, preferred_element_type=f32)
    out_ref[...] = turned * scale


def z_table(planes):
    z = np.arange(planes)
    angle = 2.0 * np.pi * ((z[:, None] * z[None, :]) % planes) / planes
    cos, sin = np.cos(angle), np.sin(angle)
    return np.stack([np.concatenate([cos, sin]), np.concatenate([-sin, cos])]).astype(jnp.bfloat16)


VMEM = pl.BlockSpec(memory_space=pltpu.VMEM)
SMEM = pl.BlockSpec(memory_space=pltpu.SMEM)
HBM = pl.BlockSpec(memory_space=pltpu.HBM)


FIRST = ((1, 0, 2, 3), (2, 3, 1, 0), (3, 2, 0, 1), (0, 1, 3, 2))
SECOND = ((1, 2, 0, 3), (2, 1, 3, 0), (3, 0, 2, 1), (0, 3, 1, 2))
FIRST_LISTED = (0, 3, 2, 1)
SECOND_LISTED = (3, 2, 1, 0)


def pairs_of(stage, slot):
    pairs = []
    for source in range(32):
        core, y, x, z = source & 1, source >> 1 & 1, source >> 2 & 1, source >> 3
        if stage == 0:
            to = FIRST[slot][2 * x + y]
            x, y = to >> 1, to & 1
        else:
            z = SECOND[slot][z]
        pairs.append((source, z << 3 | x << 2 | y << 1 | 1 - core))
    return pairs


def ctf_weights(defocus):
    x_index = jnp.arange(NX, dtype=jnp.int32)
    signed = (x_index + NX // 2) % NX - NX // 2
    y_index = jnp.arange(KY, dtype=jnp.int32) + 1
    radius = (y_index[:, None] ** 2 + signed[None, :] ** 2).astype(f32) / float(NX * NX)
    phase = 400.0 * math.pi * defocus.astype(f32)[:, None, None] * radius[None]
    return jnp.sin(phase + 0.1)


def many_planes(images, pose_bins, labels, defocus):
    owners, groups = lax.axis_size("slab"), lax.axis_size("img")
    number = images.shape[0]
    planes = owners * 4
    weighted = (ctf_weights(defocus)[:, None] * images.astype(f32)).astype(bf16)
    table = jnp.asarray(fourier_table()).reshape(QUARTERS, XBINS, LANES, 2, LANES)
    order = jnp.asarray(order_table())
    quarters = jnp.moveaxis(weighted.astype(f32).reshape(number, 2, KY, QUARTERS, LANES), 3, 0)
    sums = quarter_sums([(part[:, 0], part[:, 1]) for part in quarters])
    sums = jnp.stack([jnp.stack(pair) for pair in sums]).astype(bf16)

    def block(first_plane):
        spread = spread_matrix(pose_bins[None], labels[None], planes, first_plane)
        spread = spread.reshape(XBINS, CLASSES * PLANES, number)
        part = jnp.einsum("bci,qrikm->qrkcbm", spread, sums, preferred_element_type=f32).astype(bf16)
        both = jnp.einsum("qrkcbm,qbmsn->rsqkcn", part, table, preferred_element_type=f32)
        turned = jnp.stack([both[0, 0] - both[1, 1], both[0, 1] + both[1, 0]])
        turned = turned.reshape(2, QUARTERS, KY, CLASSES, PLANES, QUARTERS, GROUP)
        ordered = []
        for quarter in range(QUARTERS):
            groups_of = [turned[:, (j - quarter) % QUARTERS, ..., j, :] for j in range(QUARTERS)]
            value = jnp.concatenate(groups_of, axis=-1).astype(bf16)
            ordered.append(jnp.einsum("skczn,nw->kcwsz", value, order[quarter], preferred_element_type=f32))
        return jnp.stack(ordered, axis=2).astype(bf16)

    parts = lax.map(block, jnp.arange(planes // PLANES, dtype=jnp.int32) * PLANES)
    parts = jnp.moveaxis(parts, 0, -2).reshape(KY, CLASSES * NX, 2, planes).astype(f32)
    total = lax.psum_scatter(parts, "img", scatter_dimension=0, tiled=True)
    total = lax.psum_scatter(total, "slab", scatter_dimension=1, tiled=True)
    table = jnp.asarray(z_table(planes).astype(np.float32)).reshape(2, 2, planes, planes)
    scale = 2.5 / math.sqrt(number * owners * groups * NX)
    return scale * jnp.einsum("yqsz,stwz->yqtw", total, table, precision=lax.Precision.HIGHEST)


def on_device(images, pose_bins, labels, defocus):
    owners, groups = lax.axis_size("slab"), lax.axis_size("img")
    number = images.shape[0]
    planes = owners * 4
    if planes != PLANES:
        return many_planes(images, pose_bins, labels, defocus)
    scale = 2.5 / math.sqrt(number * owners * groups * NX)
    x = images.reshape(number, 2, KY, QUARTERS, LANES).transpose(0, 1, 3, 2, 4).reshape(number * 2 * ROWS, LANES)
    pieces = 2 * CLASSES * QUARTERS
    w_shape = jax.ShapeDtypeStruct((number * PITCH, LANES), f32)
    spread_shape = jax.ShapeDtypeStruct((XBINS * CLASSES * PLANES, number), bf16)
    piece_shape = jax.ShapeDtypeStruct((pieces, PLANES, 2 * LANES), bf16)
    table = jnp.asarray(fourier_table())
    table_shape = jax.ShapeDtypeStruct(table.shape, bf16)
    work = [
        pltpu.VMEM((2, number, 2 * NX), bf16),
        pltpu.VMEM((QUARTERS, 4 * CLASSES * PLANES, XBINS * LANES), bf16),
    ]
    other, weighted, spread, near_table = pl.pallas_call(
        functools.partial(first_kernel, planes),
        out_shape=(piece_shape, w_shape, spread_shape, table_shape),
        in_specs=[HBM] * 6,
        out_specs=(VMEM,) * 4,
        scratch_shapes=[
            pltpu.VMEM(x.shape, bf16),
            pltpu.VMEM((1, number), bf16),
            pltpu.VMEM((1, number), jnp.int32),
            pltpu.VMEM((1, number), jnp.int32),
            pltpu.VMEM((ROWS, LANES), f32),
            pltpu.VMEM((number, LANES), f32),
            *work,
            pltpu.SemaphoreType.DMA((CHUNKS + 5,)),
        ],
        compiler_params=pltpu.CompilerParams(vmem_limit_bytes=32 << 20),
        name="weigh_and_transform_other",
    )(*(
        pltpu.with_memory_space_constraint(v, pltpu.HBM)
        for v in (x, defocus[None], pose_bins[None], labels[None], jnp.asarray(turns_per_defocus()), table)
    ))
    axes = ("slab", "img")
    got = lax.ppermute(other, axes, [(i, i ^ 1) for i in range(owners * groups)])
    own = pl.pallas_call(
        second_kernel,
        out_shape=piece_shape,
        in_specs=[VMEM] * 3,
        out_specs=VMEM,
        scratch_shapes=work,
        compiler_params=pltpu.CompilerParams(vmem_limit_bytes=16 << 20),
        name="transform_own",
    )(weighted, spread, near_table)
    total = (own.astype(f32) + got.astype(f32)).astype(bf16)
    got = [lax.ppermute(total[4 * slot : 4 * slot + 4], axes, pairs_of(0, slot)) for slot in FIRST_LISTED]
    total = sum(g.astype(f32) for g in got).astype(bf16)
    got = [lax.ppermute(total[slot], axes, pairs_of(1, slot)) for slot in SECOND_LISTED]
    out = pl.pallas_call(
        functools.partial(last_kernel, scale),
        out_shape=jax.ShapeDtypeStruct((2 * planes, LANES), f32),
        in_specs=[VMEM] * 6,
        out_specs=VMEM,
        compiler_params=pltpu.CompilerParams(vmem_limit_bytes=16 << 20),
        name="transform_planes",
    )(*got, jnp.asarray(order_table()), jnp.asarray(z_table(planes)))
    return out.reshape(1, 2, planes, LANES).transpose(0, 3, 1, 2)


def solution(mesh):
    placed = (
        P(("slab", "img"), None, None, None),
        P(("slab", "img")),
        P(("slab", "img")),
        P(("slab", "img")),
    )
    return jax.shard_map(
        on_device, mesh=mesh, in_specs=placed, out_specs=P("img", "slab", None, None), check_vma=False
    )
```

```python
import functools
import math

import jax
import jax.numpy as jnp
import numpy as np
from jax import lax
from jax.experimental import pallas as pl
from jax.experimental.pallas import tpu as pltpu
from jax.sharding import PartitionSpec as P

NX = 512
KY = 4
CLASSES = 2
ZBINS = 4
XBINS = 4
TAPS = 8
LANES = 128
QUARTERS = NX // LANES
GROUP = LANES // QUARTERS
PLANES = 32
CHUNKS = 4
UNROLL = 8
ROWS = QUARTERS * KY
PITCH = 2 * ROWS + 1
bf16, f32 = jnp.bfloat16, jnp.float32


def lanczos_taps(num_bins):
    fraction = (np.arange(num_bins, dtype=np.float32) + np.float32(0.5)) / np.float32(num_bins)
    distance = (np.arange(TAPS, dtype=np.float32) - np.float32(3.0))[None, :] - fraction[:, None]
    kernel = (np.sinc(distance) * np.sinc(distance / np.float32(4.0))).astype(np.float32)
    return (kernel / kernel.sum(-1, keepdims=True)).astype(jnp.bfloat16).astype(np.float32)


def turns_per_defocus():
    x = np.arange(NX)
    signed = (x + NX // 2) % NX - NX // 2
    y = np.arange(KY) + 1
    radius = 200.0 * (y[:, None] ** 2 + signed[None, :] ** 2) / NX**2
    table = radius.reshape(KY, QUARTERS, LANES).transpose(1, 0, 2).reshape(ROWS, LANES)
    return table.astype(np.float32)


def fourier_table():
    taps = lanczos_taps(XBINS).astype(np.float64)
    m = np.arange(LANES)
    group, lane = np.arange(LANES) // GROUP, np.arange(LANES) % GROUP
    out = np.zeros((QUARTERS, XBINS, LANES, 2, LANES))
    for q in range(QUARTERS):
        column = 4 * (GROUP * ((group - q) % QUARTERS) + lane) + q
        shift = 2.0 * np.pi * (((np.arange(TAPS) - 3)[:, None] * column[None, :]) % NX) / NX
        wave = 2.0 * np.pi * ((m[:, None] * column[None, :]) % NX) / NX
        for b in range(XBINS):
            value = (taps[b][:, None] * np.exp(1j * shift)).sum(0)[None, :] * np.exp(1j * wave)
            out[q, b, :, 0], out[q, b, :, 1] = value.real, value.imag
    return out.reshape(QUARTERS, XBINS * LANES, 2 * LANES).astype(jnp.bfloat16)


def order_table():
    out = np.zeros((QUARTERS, LANES, LANES), np.float32)
    group, lane = np.arange(LANES) // GROUP, np.arange(LANES) % GROUP
    for quarter in range(QUARTERS):
        out[quarter, np.arange(LANES), 4 * lane + (group - quarter) % QUARTERS] = 1.0
    return out.astype(jnp.bfloat16)


def sine_coefficients(terms=5):
    f = 0.5 * np.cos(np.linspace(0.0, np.pi / 2, 4001))
    basis = f[:, None] ** (2 * np.arange(terms) + 1)
    return np.linalg.lstsq(basis, np.sin(2 * np.pi * f), rcond=None)[0].astype(np.float32)


def slot_of(schedule, here, there):
    slots = [[row[at] for row in schedule].index(there) for at in range(4)]
    slot = jnp.int32(slots[0])
    for at in range(1, 4):
        slot = jnp.where(here == at, slots[at], slot)
    return slot


def quarter_sums(parts):
    (r0, i0), (r1, i1), (r2, i2), (r3, i3) = parts
    ar, ai, br, bi = r0 + r2, i0 + i2, r0 - r2, i0 - i2
    cr, ci, dr, di = r1 + r3, i1 + i3, r1 - r3, i1 - i3
    return (ar + cr, ai + ci), (br - di, bi + dr), (ar - cr, ai - ci), (br + di, bi - dr)


def transform(w_ref, ky_low, spread, table, u_ref, v_ref, put):
    cz = CLASSES * PLANES
    number = spread.shape[1]
    for y in range(2):

        def column(r, p):
            return w_ref[pl.ds(r * ROWS + p * KY + 2 * y + ky_low, number, stride=PITCH), :]

        sums = quarter_sums([(column(0, p), column(1, p)) for p in range(QUARTERS)])
        for q in range(QUARTERS):
            for r in range(2):
                at = (r * QUARTERS + q) * LANES
                u_ref[y, :, at : at + LANES] = sums[q][r].astype(bf16)
    for y in range(2):
        part = jnp.dot(spread, u_ref[y], preferred_element_type=f32).astype(bf16)
        for r in range(2):
            for q in range(QUARTERS):
                at, row = (r * QUARTERS + q) * LANES, (r * 2 + y) * cz
                for b in range(XBINS):
                    v_ref[q, row : row + cz, b * LANES : (b + 1) * LANES] = part[b * cz : (b + 1) * cz, at : at + LANES]
    group = lax.broadcasted_iota(jnp.int32, (2 * cz, LANES), 1) // GROUP
    real, imag = [], []
    for q in range(QUARTERS):
        both = jnp.dot(v_ref[q], table(q), preferred_element_type=f32)
        real.append(both[: 2 * cz, :LANES] - both[2 * cz :, LANES:])
        imag.append(both[: 2 * cz, LANES:] + both[2 * cz :, :LANES])
    for quarter in range(QUARTERS):
        chosen = []
        for parts in (real, imag):
            value = parts[(0 - quarter) % QUARTERS]
            for j in range(1, QUARTERS):
                value = jnp.where(group == j, parts[(j - quarter) % QUARTERS], value)
            chosen.append(value.astype(bf16))
        value = jnp.concatenate(chosen, axis=1)
        for y in range(2):
            for cls in range(CLASSES):
                at = (y * CLASSES + cls) * PLANES
                put(y, cls, quarter, value[at : at + PLANES])


def spread_matrix(pose, label, planes, first_plane):
    per_pose = ZBINS * XBINS
    taps = lanczos_taps(ZBINS)
    start, zbin, xbin = pose // per_pose, pose // XBINS % ZBINS, pose % XBINS
    shape = (XBINS * CLASSES * PLANES, pose.shape[1])
    row = lax.broadcasted_iota(jnp.int32, shape, 0)
    tap = (first_plane + row % PLANES - start + planes) % planes
    tap = jnp.where(row // PLANES == xbin * CLASSES + label, tap, -1)
    out = jnp.zeros(shape, f32)
    for t in range(TAPS):
        weight = jnp.full(pose.shape, float(taps[0, t]), f32)
        for z in range(1, ZBINS):
            weight = jnp.where(zbin == z, float(taps[z, t]), weight)
        out = jnp.where(tap == t, weight, out)
    return out.astype(bf16)


def place(out_ref, core):
    slab, img = lax.axis_index("slab"), lax.axis_index("img")
    here, plane = slab % 2 * 2 + img // 2, slab // 2
    first = [
        jnp.where(core == 0, slot_of(FIRST[0], here, there), slot_of(FIRST[1], here, there)) for there in range(4)
    ]
    second = {
        schedule: [slot_of(schedule, plane, there) for there in range(4)] for schedule in dict.fromkeys(SECOND)
    }

    def put(y, cls, quarter, value):
        there = quarter % 2 * 2 + y
        out_ref[first[there] * 4 + second[SECOND[there]][cls * 2 + quarter // 2]] = value

    return put


def first_kernel(planes, x_hbm, focus_hbm, pose_hbm, label_hbm, turns_hbm, table_hbm,
                 out_ref, w_ref, spread_ref, table_ref,
                 x_ref, focus_ref, pose_ref, label_ref, turns_ref, wide_ref, u_ref, v_ref, sems):
    number = wide_ref.shape[0]
    chunk = x_ref.shape[0] // CHUNKS

    def copy(source, target, at):
        made = pltpu.make_async_copy(source, target, sems.at[at])
        made.start()
        return made

    small = [
        copy(source, target, at)
        for at, (source, target) in enumerate(
            ((focus_hbm, focus_ref), (turns_hbm, turns_ref), (pose_hbm, pose_ref), (label_hbm, label_ref))
        )
    ]
    parts = [
        copy(x_hbm.at[pl.ds(c * chunk, chunk)], x_ref.at[pl.ds(c * chunk, chunk)], 4 + c) for c in range(CHUNKS)
    ]
    table = copy(table_hbm, table_ref, 4 + CHUNKS)
    for made in small:
        made.wait()
    core = lax.axis_index("img") % 2
    coefficients = [float(v) for v in sine_coefficients()]
    wide_ref[...] = jnp.broadcast_to(focus_ref[...].astype(f32), (LANES, number)).T
    spread_ref[...] = spread_matrix(pose_ref[...], label_ref[...], planes, 0)
    turns = turns_ref[...]

    def weigh(i, carry):
        angle = turns * wide_ref[pl.ds(i, 1), :] + 0.1 / (2 * math.pi)
        f = angle - jnp.round(angle)
        square = f * f
        poly = jnp.full(f.shape, coefficients[-1], f32)
        for coefficient in coefficients[-2::-1]:
            poly = poly * square + coefficient
        ctf = poly * f
        at = pl.multiple_of(i * 2 * ROWS, 2 * ROWS)
        rows = x_ref[pl.ds(at, 2 * ROWS), :].astype(f32)
        w_ref[pl.ds(i * PITCH, ROWS), :] = ctf * rows[:ROWS]
        w_ref[pl.ds(i * PITCH + ROWS, ROWS), :] = ctf * rows[ROWS:]
        return carry

    for c in range(CHUNKS):
        parts[c].wait()
        lax.fori_loop(c * number // CHUNKS, (c + 1) * number // CHUNKS, weigh, 0, unroll=UNROLL)
    table.wait()
    transform(w_ref, 1 - core, spread_ref[...], lambda q: table_ref[q], u_ref, v_ref, place(out_ref, 1 - core))


def second_kernel(w_ref, spread_ref, table_ref, out_ref, u_ref, v_ref):
    core = lax.axis_index("img") % 2
    transform(w_ref, core, spread_ref[...], lambda q: table_ref[q], u_ref, v_ref, place(out_ref, core))


def last_kernel(scale, *refs):
    *got_refs, order_ref, table_ref, out_ref = refs
    total = sum(got_ref[...].astype(f32) for got_ref in got_refs)
    total = total.astype(bf16)
    order = order_ref[lax.axis_index("slab") % QUARTERS]
    turned = 0.0
    for s in range(2):
        part = total[:, s * LANES : (s + 1) * LANES]
        part = jnp.dot(part, order, preferred_element_type=f32).astype(bf16)
        turned += jnp.dot(table_ref[s], part, preferred_element_type=f32)
    out_ref[...] = turned * scale


def z_table(planes):
    z = np.arange(planes)
    angle = 2.0 * np.pi * ((z[:, None] * z[None, :]) % planes) / planes
    cos, sin = np.cos(angle), np.sin(angle)
    return np.stack([np.concatenate([cos, sin]), np.concatenate([-sin, cos])]).astype(jnp.bfloat16)


VMEM = pl.BlockSpec(memory_space=pltpu.VMEM)
SMEM = pl.BlockSpec(memory_space=pltpu.SMEM)
HBM = pl.BlockSpec(memory_space=pltpu.HBM)


FIRST = (((1, 0, 2, 3), (2, 3, 1, 0), (3, 2, 0, 1), (0, 1, 3, 2)),) * 2
USUAL = ((1, 2, 0, 3), (2, 1, 3, 0), (3, 0, 2, 1), (0, 3, 1, 2))
SECOND = (((1, 3, 2, 0), (2, 1, 0, 3), (3, 0, 1, 2), (0, 2, 3, 1)), USUAL, USUAL, USUAL)
FIRST_LISTED = (0, 3, 2, 1)
SECOND_LISTED = (3, 2, 1, 0)


def pairs_of(stage, slot):
    pairs = []
    for source in range(32):
        core, y, x, z = source & 1, source >> 1 & 1, source >> 2 & 1, source >> 3
        if stage == 0:
            to = FIRST[core][slot][2 * x + y]
            x, y = to >> 1, to & 1
        else:
            z = SECOND[2 * x + y][slot][z]
        pairs.append((source, z << 3 | x << 2 | y << 1 | 1 - core))
    return pairs


def ctf_weights(defocus):
    x_index = jnp.arange(NX, dtype=jnp.int32)
    signed = (x_index + NX // 2) % NX - NX // 2
    y_index = jnp.arange(KY, dtype=jnp.int32) + 1
    radius = (y_index[:, None] ** 2 + signed[None, :] ** 2).astype(f32) / float(NX * NX)
    phase = 400.0 * math.pi * defocus.astype(f32)[:, None, None] * radius[None]
    return jnp.sin(phase + 0.1)


def many_planes(images, pose_bins, labels, defocus):
    owners, groups = lax.axis_size("slab"), lax.axis_size("img")
    number = images.shape[0]
    planes = owners * 4
    weighted = (ctf_weights(defocus)[:, None] * images.astype(f32)).astype(bf16)
    table = jnp.asarray(fourier_table()).reshape(QUARTERS, XBINS, LANES, 2, LANES)
    order = jnp.asarray(order_table())
    quarters = jnp.moveaxis(weighted.astype(f32).reshape(number, 2, KY, QUARTERS, LANES), 3, 0)
    sums = quarter_sums([(part[:, 0], part[:, 1]) for part in quarters])
    sums = jnp.stack([jnp.stack(pair) for pair in sums]).astype(bf16)

    def block(first_plane):
        spread = spread_matrix(pose_bins[None], labels[None], planes, first_plane)
        spread = spread.reshape(XBINS, CLASSES * PLANES, number)
        part = jnp.einsum("bci,qrikm->qrkcbm", spread, sums, preferred_element_type=f32).astype(bf16)
        both = jnp.einsum("qrkcbm,qbmsn->rsqkcn", part, table, preferred_element_type=f32)
        turned = jnp.stack([both[0, 0] - both[1, 1], both[0, 1] + both[1, 0]])
        turned = turned.reshape(2, QUARTERS, KY, CLASSES, PLANES, QUARTERS, GROUP)
        ordered = []
        for quarter in range(QUARTERS):
            groups_of = [turned[:, (j - quarter) % QUARTERS, ..., j, :] for j in range(QUARTERS)]
            value = jnp.concatenate(groups_of, axis=-1).astype(bf16)
            ordered.append(jnp.einsum("skczn,nw->kcwsz", value, order[quarter], preferred_element_type=f32))
        return jnp.stack(ordered, axis=2).astype(bf16)

    parts = lax.map(block, jnp.arange(planes // PLANES, dtype=jnp.int32) * PLANES)
    parts = jnp.moveaxis(parts, 0, -2).reshape(KY, CLASSES * NX, 2, planes).astype(f32)
    total = lax.psum_scatter(parts, "img", scatter_dimension=0, tiled=True)
    total = lax.psum_scatter(total, "slab", scatter_dimension=1, tiled=True)
    table = jnp.asarray(z_table(planes).astype(np.float32)).reshape(2, 2, planes, planes)
    scale = 2.5 / math.sqrt(number * owners * groups * NX)
    return scale * jnp.einsum("yqsz,stwz->yqtw", total, table, precision=lax.Precision.HIGHEST)


def on_device(images, pose_bins, labels, defocus):
    owners, groups = lax.axis_size("slab"), lax.axis_size("img")
    number = images.shape[0]
    planes = owners * 4
    if planes != PLANES:
        return many_planes(images, pose_bins, labels, defocus)
    scale = 2.5 / math.sqrt(number * owners * groups * NX)
    x = images.reshape(number, 2, KY, QUARTERS, LANES).transpose(0, 1, 3, 2, 4).reshape(number * 2 * ROWS, LANES)
    pieces = 2 * CLASSES * QUARTERS
    w_shape = jax.ShapeDtypeStruct((number * PITCH, LANES), f32)
    spread_shape = jax.ShapeDtypeStruct((XBINS * CLASSES * PLANES, number), bf16)
    piece_shape = jax.ShapeDtypeStruct((pieces, PLANES, 2 * LANES), bf16)
    table = jnp.asarray(fourier_table())
    table_shape = jax.ShapeDtypeStruct(table.shape, bf16)
    work = [
        pltpu.VMEM((2, number, 2 * NX), bf16),
        pltpu.VMEM((QUARTERS, 4 * CLASSES * PLANES, XBINS * LANES), bf16),
    ]
    other, weighted, spread, near_table = pl.pallas_call(
        functools.partial(first_kernel, planes),
        out_shape=(piece_shape, w_shape, spread_shape, table_shape),
        in_specs=[HBM] * 6,
        out_specs=(VMEM,) * 4,
        scratch_shapes=[
            pltpu.VMEM(x.shape, bf16),
            pltpu.VMEM((1, number), bf16),
            pltpu.VMEM((1, number), jnp.int32),
            pltpu.VMEM((1, number), jnp.int32),
            pltpu.VMEM((ROWS, LANES), f32),
            pltpu.VMEM((number, LANES), f32),
            *work,
            pltpu.SemaphoreType.DMA((CHUNKS + 5,)),
        ],
        compiler_params=pltpu.CompilerParams(vmem_limit_bytes=32 << 20),
        name="weigh_and_transform_other",
    )(*(
        pltpu.with_memory_space_constraint(v, pltpu.HBM)
        for v in (x, defocus[None], pose_bins[None], labels[None], jnp.asarray(turns_per_defocus()), table)
    ))
    axes = ("slab", "img")
    got = lax.ppermute(other, axes, [(i, i ^ 1) for i in range(owners * groups)])
    own = pl.pallas_call(
        second_kernel,
        out_shape=piece_shape,
        in_specs=[VMEM] * 3,
        out_specs=VMEM,
        scratch_shapes=work,
        compiler_params=pltpu.CompilerParams(vmem_limit_bytes=16 << 20),
        name="transform_own",
    )(weighted, spread, near_table)
    total = (own.astype(f32) + got.astype(f32)).astype(bf16)
    got = [lax.ppermute(total[4 * slot : 4 * slot + 4], axes, pairs_of(0, slot)) for slot in FIRST_LISTED]
    total = sum(g.astype(f32) for g in got).astype(bf16)
    got = [lax.ppermute(total[slot], axes, pairs_of(1, slot)) for slot in SECOND_LISTED]
    out = pl.pallas_call(
        functools.partial(last_kernel, scale),
        out_shape=jax.ShapeDtypeStruct((2 * planes, LANES), f32),
        in_specs=[VMEM] * 6,
        out_specs=VMEM,
        compiler_params=pltpu.CompilerParams(vmem_limit_bytes=16 << 20),
        name="transform_planes",
    )(*got, jnp.asarray(order_table()), jnp.asarray(z_table(planes)))
    return out.reshape(1, 2, planes, LANES).transpose(0, 3, 1, 2)


def solution(mesh):
    placed = (
        P(("slab", "img"), None, None, None),
        P(("slab", "img")),
        P(("slab", "img")),
        P(("slab", "img")),
    )
    return jax.shard_map(
        on_device, mesh=mesh, in_specs=placed, out_specs=P("img", "slab", None, None), check_vma=False
    )
```

```python
import functools
import math

import jax
import jax.numpy as jnp
import numpy as np
from jax import lax
from jax.experimental import pallas as pl
from jax.experimental.pallas import tpu as pltpu
from jax.sharding import PartitionSpec as P

NX = 512
KY = 4
CLASSES = 2
ZBINS = 4
XBINS = 4
TAPS = 8
LANES = 128
QUARTERS = NX // LANES
GROUP = LANES // QUARTERS
PLANES = 32
CHUNKS = 4
UNROLL = 8
ROWS = QUARTERS * KY
PITCH = 2 * ROWS + 1
bf16, f32 = jnp.bfloat16, jnp.float32


def lanczos_taps(num_bins):
    fraction = (np.arange(num_bins, dtype=np.float32) + np.float32(0.5)) / np.float32(num_bins)
    distance = (np.arange(TAPS, dtype=np.float32) - np.float32(3.0))[None, :] - fraction[:, None]
    kernel = (np.sinc(distance) * np.sinc(distance / np.float32(4.0))).astype(np.float32)
    return (kernel / kernel.sum(-1, keepdims=True)).astype(jnp.bfloat16).astype(np.float32)


def turns_per_defocus():
    x = np.arange(NX)
    signed = (x + NX // 2) % NX - NX // 2
    y = np.arange(KY) + 1
    radius = 200.0 * (y[:, None] ** 2 + signed[None, :] ** 2) / NX**2
    table = radius.reshape(KY, QUARTERS, LANES).transpose(1, 0, 2).reshape(ROWS, LANES)
    return table.astype(np.float32)


def column_of(q):
    group, lane = np.arange(LANES) // GROUP, np.arange(LANES) % GROUP
    return 4 * (GROUP * ((group - q) % QUARTERS) + lane) + q


def fourier_table():
    out = np.zeros((QUARTERS, LANES, 2, LANES))
    for q in range(QUARTERS):
        wave = 2.0 * np.pi * ((np.arange(LANES)[:, None] * column_of(q)[None, :]) % NX) / NX
        out[q, :, 0], out[q, :, 1] = np.cos(wave), np.sin(wave)
    return out.reshape(QUARTERS, LANES, 2 * LANES).astype(jnp.bfloat16)


def factor_table():
    taps = lanczos_taps(XBINS).astype(np.float64)
    out = np.zeros((XBINS, QUARTERS, 2, LANES))
    for q in range(QUARTERS):
        shift = 2.0 * np.pi * (((np.arange(TAPS) - 3)[:, None] * column_of(q)[None, :]) % NX) / NX
        out[:, q, 0], out[:, q, 1] = taps @ np.cos(shift), taps @ np.sin(shift)
    return out.reshape(XBINS, 2 * NX).astype(np.float32)


def order_table():
    out = np.zeros((QUARTERS, LANES, LANES), np.float32)
    group, lane = np.arange(LANES) // GROUP, np.arange(LANES) % GROUP
    for quarter in range(QUARTERS):
        out[quarter, np.arange(LANES), 4 * lane + (group - quarter) % QUARTERS] = 1.0
    return out.astype(jnp.bfloat16)


def sine_coefficients(terms=5):
    f = 0.5 * np.cos(np.linspace(0.0, np.pi / 2, 4001))
    basis = f[:, None] ** (2 * np.arange(terms) + 1)
    return np.linalg.lstsq(basis, np.sin(2 * np.pi * f), rcond=None)[0].astype(np.float32)


def slot_of(schedule, here, there):
    slots = [[row[at] for row in schedule].index(there) for at in range(4)]
    slot = jnp.int32(slots[0])
    for at in range(1, 4):
        slot = jnp.where(here == at, slots[at], slot)
    return slot


def quarter_sums(parts):
    (r0, i0), (r1, i1), (r2, i2), (r3, i3) = parts
    ar, ai, br, bi = r0 + r2, i0 + i2, r0 - r2, i0 - i2
    cr, ci, dr, di = r1 + r3, i1 + i3, r1 - r3, i1 - i3
    return (ar + cr, ai + ci), (br - di, bi + dr), (ar - cr, ai - ci), (br + di, bi - dr)


def transform(w_ref, ky_low, spread_ref, table_ref, factor_ref, u_ref, v_ref, put):
    number = spread_ref.shape[1]
    for y in range(2):

        def column(r, p):
            return w_ref[pl.ds(r * ROWS + p * KY + 2 * y + ky_low, number, stride=PITCH), :]

        sums = quarter_sums([(column(0, p), column(1, p)) for p in range(QUARTERS)])
        for q in range(QUARTERS):
            for r in range(2):
                at = (r * 2 + y) * number
                u_ref[q, at : at + number, :] = sums[q][r].astype(bf16)
    for q in range(QUARTERS):
        both = jnp.dot(u_ref[q], table_ref[q], preferred_element_type=f32)
        real = both[: 2 * number, :LANES] - both[2 * number :, LANES:]
        imag = both[: 2 * number, LANES:] + both[2 * number :, :LANES]
        by_real, by_imag = (factor_ref[:, (2 * q + s) * LANES : (2 * q + s + 1) * LANES] for s in range(2))
        for y in range(2):
            rows = slice(y * number, (y + 1) * number)
            at = (y * QUARTERS + q) * 2 * LANES
            v_ref[:, at : at + LANES] = (real[rows] * by_real - imag[rows] * by_imag).astype(bf16)
            v_ref[:, at + LANES : at + 2 * LANES] = (real[rows] * by_imag + imag[rows] * by_real).astype(bf16)
    group = lax.broadcasted_iota(jnp.int32, (CLASSES * PLANES, 2 * LANES), 1) % LANES // GROUP
    for y in range(2):
        part = jnp.dot(
            spread_ref[...], v_ref[:, y * 2 * NX : (y + 1) * 2 * NX], preferred_element_type=f32
        )
        parts = [part[:, q * 2 * LANES : (q + 1) * 2 * LANES] for q in range(QUARTERS)]
        for quarter in range(QUARTERS):
            value = parts[-quarter % QUARTERS]
            for j in range(1, QUARTERS):
                value = jnp.where(group == j, parts[(j - quarter) % QUARTERS], value)
            value = value.astype(bf16)
            for cls in range(CLASSES):
                put(y, cls, quarter, value[cls * PLANES : (cls + 1) * PLANES])


def spread_matrix(pose, label, planes, first_plane):
    per_pose = ZBINS * XBINS
    taps = lanczos_taps(ZBINS)
    start, zbin = pose // per_pose, pose // XBINS % ZBINS
    shape = (CLASSES * PLANES, pose.shape[1])
    row = lax.broadcasted_iota(jnp.int32, shape, 0)
    tap = (first_plane + row % PLANES - start + planes) % planes
    tap = jnp.where(row // PLANES == label, tap, -1)
    out = jnp.zeros(shape, f32)
    for t in range(TAPS):
        weight = jnp.full(pose.shape, float(taps[0, t]), f32)
        for z in range(1, ZBINS):
            weight = jnp.where(zbin == z, float(taps[z, t]), weight)
        out = jnp.where(tap == t, weight, out)
    return out.astype(bf16)


def place(out_ref, core):
    slab, img = lax.axis_index("slab"), lax.axis_index("img")
    here, plane = slab % 2 * 2 + img // 2, slab // 2
    first = [
        jnp.where(core == 0, slot_of(FIRST[0], here, there), slot_of(FIRST[1], here, there)) for there in range(4)
    ]
    second = {
        schedule: [slot_of(schedule, plane, there) for there in range(4)] for schedule in dict.fromkeys(SECOND)
    }

    def put(y, cls, quarter, value):
        there = quarter % 2 * 2 + y
        out_ref[first[there] * 4 + second[SECOND[there]][cls * 2 + quarter // 2]] = value

    return put


def first_kernel(planes, x_hbm, focus_hbm, pose_hbm, label_hbm, turns_hbm, bins_hbm, table_hbm,
                 out_ref, w_ref, spread_ref, table_ref, factor_ref,
                 x_ref, focus_ref, pose_ref, label_ref, turns_ref, bins_ref, wide_ref, u_ref, v_ref, sems):
    number = wide_ref.shape[0]
    chunk = x_ref.shape[0] // CHUNKS

    def copy(source, target, at):
        made = pltpu.make_async_copy(source, target, sems.at[at])
        made.start()
        return made

    small = [
        copy(source, target, at)
        for at, (source, target) in enumerate(
            (
                (focus_hbm, focus_ref),
                (turns_hbm, turns_ref),
                (pose_hbm, pose_ref),
                (label_hbm, label_ref),
                (bins_hbm, bins_ref),
            )
        )
    ]
    parts = [
        copy(x_hbm.at[pl.ds(c * chunk, chunk)], x_ref.at[pl.ds(c * chunk, chunk)], 5 + c) for c in range(CHUNKS)
    ]
    table = copy(table_hbm, table_ref, 5 + CHUNKS)
    for made in small:
        made.wait()
    core = lax.axis_index("img") % 2
    coefficients = [float(v) for v in sine_coefficients()]
    wide_ref[...] = jnp.broadcast_to(focus_ref[...].astype(f32), (LANES, number)).T
    spread_ref[...] = spread_matrix(pose_ref[...], label_ref[...], planes, 0)
    xbin = jnp.broadcast_to((pose_ref[...] % XBINS).astype(f32), (LANES, number)).T
    for at in range(0, 2 * NX, LANES):
        chosen = bins_ref[0:1, at : at + LANES]
        for b in range(1, XBINS):
            chosen = jnp.where(xbin == b, bins_ref[b : b + 1, at : at + LANES], chosen)
        factor_ref[:, at : at + LANES] = chosen
    turns = turns_ref[...]

    def weigh(i, carry):
        angle = turns * wide_ref[pl.ds(i, 1), :] + 0.1 / (2 * math.pi)
        f = angle - jnp.round(angle)
        square = f * f
        poly = jnp.full(f.shape, coefficients[-1], f32)
        for coefficient in coefficients[-2::-1]:
            poly = poly * square + coefficient
        ctf = poly * f
        at = pl.multiple_of(i * 2 * ROWS, 2 * ROWS)
        rows = x_ref[pl.ds(at, 2 * ROWS), :].astype(f32)
        w_ref[pl.ds(i * PITCH, ROWS), :] = ctf * rows[:ROWS]
        w_ref[pl.ds(i * PITCH + ROWS, ROWS), :] = ctf * rows[ROWS:]
        return carry

    for c in range(CHUNKS):
        parts[c].wait()
        lax.fori_loop(c * number // CHUNKS, (c + 1) * number // CHUNKS, weigh, 0, unroll=UNROLL)
    table.wait()
    transform(w_ref, 1 - core, spread_ref, table_ref, factor_ref, u_ref, v_ref, place(out_ref, 1 - core))


def second_kernel(w_ref, spread_ref, table_ref, factor_ref, out_ref, u_ref, v_ref):
    core = lax.axis_index("img") % 2
    transform(w_ref, core, spread_ref, table_ref, factor_ref, u_ref, v_ref, place(out_ref, core))


def last_kernel(scale, *refs):
    *got_refs, order_ref, table_ref, out_ref = refs
    total = sum(got_ref[...].astype(f32) for got_ref in got_refs)
    total = total.astype(bf16)
    order = order_ref[lax.axis_index("slab") % QUARTERS]
    turned = 0.0
    for s in range(2):
        part = total[:, s * LANES : (s + 1) * LANES]
        part = jnp.dot(part, order, preferred_element_type=f32).astype(bf16)
        turned += jnp.dot(table_ref[s], part, preferred_element_type=f32)
    out_ref[...] = turned * scale


def z_table(planes):
    z = np.arange(planes)
    angle = 2.0 * np.pi * ((z[:, None] * z[None, :]) % planes) / planes
    cos, sin = np.cos(angle), np.sin(angle)
    return np.stack([np.concatenate([cos, sin]), np.concatenate([-sin, cos])]).astype(jnp.bfloat16)


VMEM = pl.BlockSpec(memory_space=pltpu.VMEM)
SMEM = pl.BlockSpec(memory_space=pltpu.SMEM)
HBM = pl.BlockSpec(memory_space=pltpu.HBM)


FIRST = (((1, 0, 2, 3), (2, 3, 1, 0), (3, 2, 0, 1), (0, 1, 3, 2)),) * 2
USUAL = ((1, 2, 0, 3), (2, 1, 3, 0), (3, 0, 2, 1), (0, 3, 1, 2))
SECOND = (((1, 3, 2, 0), (2, 1, 0, 3), (3, 0, 1, 2), (0, 2, 3, 1)), USUAL, USUAL, USUAL)
FIRST_LISTED = (0, 3, 2, 1)
SECOND_LISTED = (3, 2, 1, 0)


def pairs_of(stage, slot):
    pairs = []
    for source in range(32):
        core, y, x, z = source & 1, source >> 1 & 1, source >> 2 & 1, source >> 3
        if stage == 0:
            to = FIRST[core][slot][2 * x + y]
            x, y = to >> 1, to & 1
        else:
            z = SECOND[2 * x + y][slot][z]
        pairs.append((source, z << 3 | x << 2 | y << 1 | 1 - core))
    return pairs


def ctf_weights(defocus):
    x_index = jnp.arange(NX, dtype=jnp.int32)
    signed = (x_index + NX // 2) % NX - NX // 2
    y_index = jnp.arange(KY, dtype=jnp.int32) + 1
    radius = (y_index[:, None] ** 2 + signed[None, :] ** 2).astype(f32) / float(NX * NX)
    phase = 400.0 * math.pi * defocus.astype(f32)[:, None, None] * radius[None]
    return jnp.sin(phase + 0.1)


def many_planes(images, pose_bins, labels, defocus):
    owners, groups = lax.axis_size("slab"), lax.axis_size("img")
    number = images.shape[0]
    planes = owners * 4
    weighted = (ctf_weights(defocus)[:, None] * images.astype(f32)).astype(bf16)
    table = jnp.asarray(fourier_table()).reshape(QUARTERS, LANES, 2, LANES)
    factors = jnp.asarray(factor_table()).reshape(XBINS, QUARTERS, 2, LANES)[pose_bins % XBINS]
    by_real, by_imag = (jnp.moveaxis(factors[:, :, s], 0, 1)[:, :, None] for s in range(2))
    quarters = jnp.moveaxis(weighted.astype(f32).reshape(number, 2, KY, QUARTERS, LANES), 3, 0)
    sums = quarter_sums([(part[:, 0], part[:, 1]) for part in quarters])
    sums = jnp.stack([jnp.stack(pair) for pair in sums]).astype(bf16)
    both = jnp.einsum("qrikm,qmsn->rsqikn", sums, table, preferred_element_type=f32)
    real, imag = both[0, 0] - both[1, 1], both[0, 1] + both[1, 0]
    turned = jnp.stack([real * by_real - imag * by_imag, real * by_imag + imag * by_real]).astype(bf16)
    columns = np.argsort(np.concatenate([column_of(q) for q in range(QUARTERS)]))
    turned = jnp.moveaxis(turned, 1, 3).reshape(2, number, KY, NX)[..., columns]

    def block(first_plane):
        spread = spread_matrix(pose_bins[None], labels[None], planes, first_plane)
        spread = spread.reshape(CLASSES, PLANES, number)
        return jnp.einsum("czi,sikx->kcxsz", spread, turned, preferred_element_type=f32).astype(bf16)

    parts = lax.map(block, jnp.arange(planes // PLANES, dtype=jnp.int32) * PLANES)
    parts = jnp.moveaxis(parts, 0, -2).reshape(KY, CLASSES * NX, 2, planes).astype(f32)
    total = lax.psum_scatter(parts, "img", scatter_dimension=0, tiled=True)
    total = lax.psum_scatter(total, "slab", scatter_dimension=1, tiled=True)
    table = jnp.asarray(z_table(planes).astype(np.float32)).reshape(2, 2, planes, planes)
    scale = 2.5 / math.sqrt(number * owners * groups * NX)
    return scale * jnp.einsum("yqsz,stwz->yqtw", total, table, precision=lax.Precision.HIGHEST)


def on_device(images, pose_bins, labels, defocus):
    owners, groups = lax.axis_size("slab"), lax.axis_size("img")
    number = images.shape[0]
    planes = owners * 4
    if planes != PLANES:
        return many_planes(images, pose_bins, labels, defocus)
    scale = 2.5 / math.sqrt(number * owners * groups * NX)
    x = images.reshape(number, 2, KY, QUARTERS, LANES).transpose(0, 1, 3, 2, 4).reshape(number * 2 * ROWS, LANES)
    pieces = 2 * CLASSES * QUARTERS
    w_shape = jax.ShapeDtypeStruct((number * PITCH, LANES), f32)
    spread_shape = jax.ShapeDtypeStruct((CLASSES * PLANES, number), bf16)
    piece_shape = jax.ShapeDtypeStruct((pieces, PLANES, 2 * LANES), bf16)
    table = jnp.asarray(fourier_table())
    table_shape = jax.ShapeDtypeStruct(table.shape, bf16)
    bins = jnp.asarray(factor_table())
    factor_shape = jax.ShapeDtypeStruct((number, 2 * NX), f32)
    work = [pltpu.VMEM((QUARTERS, 4 * number, LANES), bf16), pltpu.VMEM((number, 4 * NX), bf16)]
    other, *near = pl.pallas_call(
        functools.partial(first_kernel, planes),
        out_shape=(piece_shape, w_shape, spread_shape, table_shape, factor_shape),
        in_specs=[HBM] * 7,
        out_specs=(VMEM,) * 5,
        scratch_shapes=[
            pltpu.VMEM(x.shape, bf16),
            pltpu.VMEM((1, number), bf16),
            pltpu.VMEM((1, number), jnp.int32),
            pltpu.VMEM((1, number), jnp.int32),
            pltpu.VMEM((ROWS, LANES), f32),
            pltpu.VMEM(bins.shape, f32),
            pltpu.VMEM((number, LANES), f32),
            *work,
            pltpu.SemaphoreType.DMA((CHUNKS + 6,)),
        ],
        compiler_params=pltpu.CompilerParams(vmem_limit_bytes=32 << 20),
        name="weigh_and_transform_other",
    )(*(
        pltpu.with_memory_space_constraint(v, pltpu.HBM)
        for v in (x, defocus[None], pose_bins[None], labels[None], jnp.asarray(turns_per_defocus()), bins, table)
    ))
    axes = ("slab", "img")
    got = lax.ppermute(other, axes, [(i, i ^ 1) for i in range(owners * groups)])
    own = pl.pallas_call(
        second_kernel,
        out_shape=piece_shape,
        in_specs=[VMEM] * 4,
        out_specs=VMEM,
        scratch_shapes=work,
        compiler_params=pltpu.CompilerParams(vmem_limit_bytes=16 << 20),
        name="transform_own",
    )(*near)
    total = (own.astype(f32) + got.astype(f32)).astype(bf16)
    got = [lax.ppermute(total[4 * slot : 4 * slot + 4], axes, pairs_of(0, slot)) for slot in FIRST_LISTED]
    total = sum(g.astype(f32) for g in got).astype(bf16)
    got = [lax.ppermute(total[slot], axes, pairs_of(1, slot)) for slot in SECOND_LISTED]
    out = pl.pallas_call(
        functools.partial(last_kernel, scale),
        out_shape=jax.ShapeDtypeStruct((2 * planes, LANES), f32),
        in_specs=[VMEM] * 6,
        out_specs=VMEM,
        compiler_params=pltpu.CompilerParams(vmem_limit_bytes=16 << 20),
        name="transform_planes",
    )(*got, jnp.asarray(order_table()), jnp.asarray(z_table(planes)))
    return out.reshape(1, 2, planes, LANES).transpose(0, 3, 1, 2)


def solution(mesh):
    placed = (
        P(("slab", "img"), None, None, None),
        P(("slab", "img")),
        P(("slab", "img")),
        P(("slab", "img")),
    )
    return jax.shard_map(
        on_device, mesh=mesh, in_specs=placed, out_specs=P("img", "slab", None, None), check_vma=False
    )
```

```python
import functools
import math

import jax
import jax.numpy as jnp
import numpy as np
from jax import lax
from jax.experimental import pallas as pl
from jax.experimental.pallas import tpu as pltpu
from jax.sharding import PartitionSpec as P

NX = 512
KY = 4
CLASSES = 2
ZBINS = 4
XBINS = 4
TAPS = 8
LANES = 128
QUARTERS = NX // LANES
PLANES = 32
CHUNKS = 4
UNROLL = 16
PARTS = 4
ROWS = QUARTERS * KY
PITCH = 2 * ROWS + 1
bf16, f32 = jnp.bfloat16, jnp.float32


def lanczos_taps(num_bins):
    fraction = (np.arange(num_bins, dtype=np.float32) + np.float32(0.5)) / np.float32(num_bins)
    distance = (np.arange(TAPS, dtype=np.float32) - np.float32(3.0))[None, :] - fraction[:, None]
    kernel = (np.sinc(distance) * np.sinc(distance / np.float32(4.0))).astype(np.float32)
    return (kernel / kernel.sum(-1, keepdims=True)).astype(jnp.bfloat16).astype(np.float32)


def turns_per_defocus():
    x = np.arange(NX)
    signed = (x + NX // 2) % NX - NX // 2
    y = np.arange(KY) + 1
    radius = 200.0 * (y[:, None] ** 2 + signed[None, :] ** 2) / NX**2
    table = radius.reshape(KY, QUARTERS, LANES).transpose(1, 0, 2).reshape(ROWS, LANES)
    return table.astype(np.float32)


def column_of(q):
    place = np.arange(LANES)
    quarter = (place - q) % QUARTERS
    return 4 * (LANES // QUARTERS * quarter + (place - q - quarter) % LANES // 4) + q


def fourier_table():
    out = np.zeros((QUARTERS, LANES, 2, LANES))
    for q in range(QUARTERS):
        wave = 2.0 * np.pi * ((np.arange(LANES)[:, None] * column_of(q)[None, :]) % NX) / NX
        out[q, :, 0], out[q, :, 1] = np.cos(wave), np.sin(wave)
    return out.reshape(QUARTERS, LANES, 2 * LANES).astype(jnp.bfloat16)


def factor_table(scale):
    taps = scale * lanczos_taps(XBINS).astype(np.float64)
    out = np.zeros((XBINS, QUARTERS, 2, LANES))
    for q in range(QUARTERS):
        shift = 2.0 * np.pi * (((np.arange(TAPS) - 3)[:, None] * column_of(q)[None, :]) % NX) / NX
        out[:, q, 0], out[:, q, 1] = taps @ np.cos(shift), taps @ np.sin(shift)
    return out.reshape(XBINS, 2 * NX).astype(np.float32)


def z_table(planes):
    z = np.arange(planes)
    angle = 2.0 * np.pi * ((z[:, None] * z[None, :]) % planes) / planes
    cos, sin = np.cos(angle), np.sin(angle)
    return np.stack([np.concatenate([cos, sin]), np.concatenate([-sin, cos])])


def sine_coefficients(terms=5):
    f = 0.5 * np.cos(np.linspace(0.0, np.pi / 2, 4001))
    basis = f[:, None] ** (2 * np.arange(terms) + 1)
    return np.linalg.lstsq(basis, np.sin(2 * np.pi * f), rcond=None)[0].astype(np.float32)


def slot_of(schedule, here, there):
    slots = [[row[at] for row in schedule].index(there) for at in range(4)]
    slot = jnp.int32(slots[0])
    for at in range(1, 4):
        slot = jnp.where(here == at, slots[at], slot)
    return slot


def quarter_sums(parts):
    (r0, i0), (r1, i1), (r2, i2), (r3, i3) = parts
    ar, ai, br, bi = r0 + r2, i0 + i2, r0 - r2, i0 - i2
    cr, ci, dr, di = r1 + r3, i1 + i3, r1 - r3, i1 - i3
    return (ar + cr, ai + ci), (br - di, bi + dr), (ar - cr, ai - ci), (br + di, bi - dr)


def transform(w_ref, ky_low, spread_ref, table_ref, factor_ref, v_ref, put):
    number = spread_ref.shape[1] // 2
    count = number // PARTS
    for at in range(0, number, count):
        sums = []
        for y in range(2):

            def column(r, p):
                return w_ref[pl.ds(at * PITCH + r * ROWS + p * KY + 2 * y + ky_low, count, stride=PITCH), :]

            sums.append(quarter_sums([(column(0, p), column(1, p)) for p in range(QUARTERS)]))
        for q in range(QUARTERS):
            rows = jnp.concatenate([sums[y][q][r] for r in range(2) for y in range(2)], axis=0).astype(bf16)
            both = jnp.dot(rows, table_ref[q], preferred_element_type=f32)
            real = both[: 2 * count, :LANES] - both[2 * count :, LANES:]
            imag = both[: 2 * count, LANES:] + both[2 * count :, :LANES]
            by_real, by_imag = (
                factor_ref[at : at + count, (2 * q + s) * LANES : (2 * q + s + 1) * LANES] for s in range(2)
            )
            for y in range(2):
                part = slice(y * count, (y + 1) * count)
                to = slice((y * QUARTERS + q) * LANES, (y * QUARTERS + q + 1) * LANES)
                v_ref[at : at + count, to] = (real[part] * by_real - imag[part] * by_imag).astype(bf16)
                v_ref[number + at : number + at + count, to] = (
                    real[part] * by_imag + imag[part] * by_real
                ).astype(bf16)
    group = lax.broadcasted_iota(jnp.int32, (CLASSES * 2 * PLANES, LANES), 1) % QUARTERS
    for y in range(2):
        part = jnp.dot(spread_ref[...], v_ref[:, y * NX : (y + 1) * NX], preferred_element_type=f32)
        parts = [part[:, q * LANES : (q + 1) * LANES] for q in range(QUARTERS)]
        for quarter in range(QUARTERS):
            value = parts[-quarter % QUARTERS]
            for j in range(1, QUARTERS):
                value = jnp.where(group == j, parts[(j - quarter) % QUARTERS], value)
            value = value.astype(bf16)
            for cls in range(CLASSES):
                put(y, cls, quarter, value[cls * 2 * PLANES : (cls + 1) * 2 * PLANES])


def spread_matrix(pose, label, planes, first_plane):
    per_pose = ZBINS * XBINS
    taps = lanczos_taps(ZBINS)
    start, zbin = pose // per_pose, pose // XBINS % ZBINS
    shape = (CLASSES * PLANES, pose.shape[1])
    row = lax.broadcasted_iota(jnp.int32, shape, 0)
    tap = (first_plane + row % PLANES - start + planes) % planes
    tap = jnp.where(row // PLANES == label, tap, -1)
    out = jnp.zeros(shape, f32)
    for t in range(TAPS):
        weight = jnp.full(pose.shape, float(taps[0, t]), f32)
        for z in range(1, ZBINS):
            weight = jnp.where(zbin == z, float(taps[z, t]), weight)
        out = jnp.where(tap == t, weight, out)
    return out.astype(bf16)


def place(out_ref, core):
    slab, img = lax.axis_index("slab"), lax.axis_index("img")
    here, plane = slab % 2 * 2 + img // 2, slab // 2
    first = [
        jnp.where(core == 0, slot_of(FIRST[0], here, there), slot_of(FIRST[1], here, there)) for there in range(4)
    ]
    second = {
        schedule: [slot_of(schedule, plane, there) for there in range(4)] for schedule in dict.fromkeys(SECOND)
    }

    def put(y, cls, quarter, value):
        there = quarter % 2 * 2 + y
        out_ref[first[there] * 4 + second[SECOND[there]][cls * 2 + quarter // 2]] = value

    return put


def first_kernel(planes, x_hbm, focus_hbm, pose_hbm, label_hbm, turns_hbm, bins_hbm, along_z_hbm, table_hbm,
                 out_ref, w_ref, spread_ref, table_ref, factor_ref,
                 x_ref, focus_ref, pose_ref, label_ref, turns_ref, bins_ref, along_z_ref, wide_ref, v_ref, sems):
    number = wide_ref.shape[0]
    chunk = x_ref.shape[0] // CHUNKS

    def copy(source, target, at):
        made = pltpu.make_async_copy(source, target, sems.at[at])
        made.start()
        return made

    small = [
        copy(source, target, at)
        for at, (source, target) in enumerate(
            (
                (focus_hbm, focus_ref),
                (turns_hbm, turns_ref),
                (pose_hbm, pose_ref),
                (label_hbm, label_ref),
                (bins_hbm, bins_ref),
                (along_z_hbm, along_z_ref),
            )
        )
    ]
    parts = [
        copy(x_hbm.at[pl.ds(c * chunk, chunk)], x_ref.at[pl.ds(c * chunk, chunk)], 6 + c) for c in range(CHUNKS)
    ]
    table = copy(table_hbm, table_ref, 6 + CHUNKS)
    for made in small:
        made.wait()
    core = lax.axis_index("img") % 2
    coefficients = [float(v) for v in sine_coefficients()]
    wide_ref[...] = jnp.broadcast_to(focus_ref[...].astype(f32), (LANES, number)).T
    planar = spread_matrix(pose_ref[...], label_ref[...], planes, 0)
    xbin = jnp.broadcast_to((pose_ref[...] % XBINS).astype(f32), (LANES, number)).T
    for at in range(0, 2 * NX, LANES):
        chosen = bins_ref[0:1, at : at + LANES]
        for b in range(1, XBINS):
            chosen = jnp.where(xbin == b, bins_ref[b : b + 1, at : at + LANES], chosen)
        factor_ref[:, at : at + LANES] = chosen
    turns = turns_ref[...]

    def weigh(i, carry):
        angle = turns * wide_ref[pl.ds(i, 1), :] + 0.1 / (2 * math.pi)
        f = angle - jnp.round(angle)
        square = f * f
        poly = jnp.full(f.shape, coefficients[-1], f32)
        for coefficient in coefficients[-2::-1]:
            poly = poly * square + coefficient
        ctf = poly * f
        at = pl.multiple_of(i * 2 * ROWS, 2 * ROWS)
        rows = x_ref[pl.ds(at, 2 * ROWS), :].astype(f32)
        w_ref[pl.ds(i * PITCH, ROWS), :] = ctf * rows[:ROWS]
        w_ref[pl.ds(i * PITCH + ROWS, ROWS), :] = ctf * rows[ROWS:]
        return carry

    for c in range(CHUNKS):
        parts[c].wait()
        lax.fori_loop(c * number // CHUNKS, (c + 1) * number // CHUNKS, weigh, 0, unroll=UNROLL)
    table.wait()
    for s in range(2):
        spread = jnp.dot(along_z_ref[s], planar, preferred_element_type=f32).astype(bf16)
        spread_ref[:, s * number : (s + 1) * number] = spread
    transform(w_ref, 1 - core, spread_ref, table_ref, factor_ref, v_ref, place(out_ref, 1 - core))


def second_kernel(w_ref, spread_ref, table_ref, factor_ref, out_ref, v_ref):
    core = lax.axis_index("img") % 2
    transform(w_ref, core, spread_ref, table_ref, factor_ref, v_ref, place(out_ref, core))


def last_kernel(*refs):
    *got_refs, out_ref = refs
    quarter = lax.axis_index("slab") % QUARTERS
    total = sum(got_ref[...].astype(f32) for got_ref in got_refs)
    out_ref[...] = pltpu.roll(total, (LANES - quarter) % LANES, 1)


VMEM = pl.BlockSpec(memory_space=pltpu.VMEM)
SMEM = pl.BlockSpec(memory_space=pltpu.SMEM)
HBM = pl.BlockSpec(memory_space=pltpu.HBM)


FIRST = (((1, 0, 2, 3), (2, 3, 1, 0), (3, 2, 0, 1), (0, 1, 3, 2)),) * 2
USUAL = ((1, 2, 0, 3), (2, 1, 3, 0), (3, 0, 2, 1), (0, 3, 1, 2))
SECOND = (((1, 3, 2, 0), (2, 1, 0, 3), (3, 0, 1, 2), (0, 2, 3, 1)), USUAL, USUAL, USUAL)
FIRST_LISTED = (0, 3, 2, 1)
SECOND_LISTED = (3, 2, 1, 0)


def pairs_of(stage, slot):
    pairs = []
    for source in range(32):
        core, y, x, z = source & 1, source >> 1 & 1, source >> 2 & 1, source >> 3
        if stage == 0:
            to = FIRST[core][slot][2 * x + y]
            x, y = to >> 1, to & 1
        else:
            z = SECOND[2 * x + y][slot][z]
        pairs.append((source, z << 3 | x << 2 | y << 1 | 1 - core))
    return pairs


def ctf_weights(defocus):
    x_index = jnp.arange(NX, dtype=jnp.int32)
    signed = (x_index + NX // 2) % NX - NX // 2
    y_index = jnp.arange(KY, dtype=jnp.int32) + 1
    radius = (y_index[:, None] ** 2 + signed[None, :] ** 2).astype(f32) / float(NX * NX)
    phase = 400.0 * math.pi * defocus.astype(f32)[:, None, None] * radius[None]
    return jnp.sin(phase + 0.1)


def many_planes(images, pose_bins, labels, defocus):
    owners, groups = lax.axis_size("slab"), lax.axis_size("img")
    number = images.shape[0]
    planes = owners * 4
    weighted = (ctf_weights(defocus)[:, None] * images.astype(f32)).astype(bf16)
    table = jnp.asarray(fourier_table()).reshape(QUARTERS, LANES, 2, LANES)
    scale = 2.5 / math.sqrt(number * owners * groups * NX)
    factors = jnp.asarray(factor_table(scale)).reshape(XBINS, QUARTERS, 2, LANES)[pose_bins % XBINS]
    by_real, by_imag = (jnp.moveaxis(factors[:, :, s], 0, 1)[:, :, None] for s in range(2))
    quarters = jnp.moveaxis(weighted.astype(f32).reshape(number, 2, KY, QUARTERS, LANES), 3, 0)
    sums = quarter_sums([(part[:, 0], part[:, 1]) for part in quarters])
    sums = jnp.stack([jnp.stack(pair) for pair in sums]).astype(bf16)
    both = jnp.einsum("qrikm,qmsn->rsqikn", sums, table, preferred_element_type=f32)
    real, imag = both[0, 0] - both[1, 1], both[0, 1] + both[1, 0]
    turned = jnp.stack([real * by_real - imag * by_imag, real * by_imag + imag * by_real]).astype(bf16)
    columns = np.argsort(np.concatenate([column_of(q) for q in range(QUARTERS)]))
    turned = jnp.moveaxis(turned, 1, 3).reshape(2, number, KY, NX)[..., columns]

    def block(first_plane):
        spread = spread_matrix(pose_bins[None], labels[None], planes, first_plane)
        spread = spread.reshape(CLASSES, PLANES, number)
        return jnp.einsum("czi,sikx->kcxsz", spread, turned, preferred_element_type=f32).astype(bf16)

    parts = lax.map(block, jnp.arange(planes // PLANES, dtype=jnp.int32) * PLANES)
    parts = jnp.moveaxis(parts, 0, -2).reshape(KY, CLASSES * NX, 2, planes).astype(f32)
    total = lax.psum_scatter(parts, "img", scatter_dimension=0, tiled=True)
    total = lax.psum_scatter(total, "slab", scatter_dimension=1, tiled=True)
    table = jnp.asarray(z_table(planes).astype(np.float32)).reshape(2, 2, planes, planes)
    return jnp.einsum("yqsz,stwz->yqtw", total, table, precision=lax.Precision.HIGHEST)


def on_device(images, pose_bins, labels, defocus):
    owners, groups = lax.axis_size("slab"), lax.axis_size("img")
    number = images.shape[0]
    planes = owners * 4
    if planes != PLANES:
        return many_planes(images, pose_bins, labels, defocus)
    scale = 2.5 / math.sqrt(number * owners * groups * NX)
    x = images.reshape(number, 2, KY, QUARTERS, LANES).transpose(0, 1, 3, 2, 4).reshape(number * 2 * ROWS, LANES)
    pieces = 2 * CLASSES * QUARTERS
    w_shape = jax.ShapeDtypeStruct((number * PITCH, LANES), f32)
    spread_shape = jax.ShapeDtypeStruct((CLASSES * 2 * PLANES, 2 * number), bf16)
    piece_shape = jax.ShapeDtypeStruct((pieces, 2 * PLANES, LANES), bf16)
    table = jnp.asarray(fourier_table())
    table_shape = jax.ShapeDtypeStruct(table.shape, bf16)
    bins = jnp.asarray(factor_table(scale))
    along_z = jnp.asarray(np.stack([np.kron(np.eye(CLASSES), part) for part in z_table(planes)]).astype(jnp.bfloat16))
    factor_shape = jax.ShapeDtypeStruct((number, 2 * NX), f32)
    work = [pltpu.VMEM((2 * number, 2 * NX), bf16)]
    other, *near = pl.pallas_call(
        functools.partial(first_kernel, planes),
        out_shape=(piece_shape, w_shape, spread_shape, table_shape, factor_shape),
        in_specs=[HBM] * 8,
        out_specs=(VMEM,) * 5,
        scratch_shapes=[
            pltpu.VMEM(x.shape, bf16),
            pltpu.VMEM((1, number), bf16),
            pltpu.VMEM((1, number), jnp.int32),
            pltpu.VMEM((1, number), jnp.int32),
            pltpu.VMEM((ROWS, LANES), f32),
            pltpu.VMEM(bins.shape, f32),
            pltpu.VMEM(along_z.shape, bf16),
            pltpu.VMEM((number, LANES), f32),
            *work,
            pltpu.SemaphoreType.DMA((CHUNKS + 7,)),
        ],
        compiler_params=pltpu.CompilerParams(vmem_limit_bytes=32 << 20),
        name="weigh_and_transform_other",
    )(*(
        pltpu.with_memory_space_constraint(v, pltpu.HBM)
        for v in (x, defocus[None], pose_bins[None], labels[None], jnp.asarray(turns_per_defocus()), bins, along_z, table)
    ))
    axes = ("slab", "img")
    got = lax.ppermute(other, axes, [(i, i ^ 1) for i in range(owners * groups)])
    own = pl.pallas_call(
        second_kernel,
        out_shape=piece_shape,
        in_specs=[VMEM] * 4,
        out_specs=VMEM,
        scratch_shapes=work,
        compiler_params=pltpu.CompilerParams(vmem_limit_bytes=16 << 20),
        name="transform_own",
    )(*near)
    total = (own.astype(f32) + got.astype(f32)).astype(bf16)
    got = [lax.ppermute(total[4 * slot : 4 * slot + 4], axes, pairs_of(0, slot)) for slot in FIRST_LISTED]
    total = sum(g.astype(f32) for g in got).astype(bf16)
    got = [lax.ppermute(total[slot], axes, pairs_of(1, slot)) for slot in SECOND_LISTED]
    out = pl.pallas_call(
        last_kernel,
        out_shape=jax.ShapeDtypeStruct((2 * planes, LANES), f32),
        in_specs=[VMEM] * 4,
        out_specs=VMEM,
        compiler_params=pltpu.CompilerParams(vmem_limit_bytes=16 << 20),
        name="add_last",
    )(*got)
    return out.reshape(1, 2, planes, LANES).transpose(0, 3, 1, 2)


def solution(mesh):
    placed = (
        P(("slab", "img"), None, None, None),
        P(("slab", "img")),
        P(("slab", "img")),
        P(("slab", "img")),
    )
    return jax.shard_map(
        on_device, mesh=mesh, in_specs=placed, out_specs=P("img", "slab", None, None), check_vma=False
    )
```

```python
import functools
import math

import jax
import jax.numpy as jnp
import numpy as np
from jax import lax
from jax.experimental import pallas as pl
from jax.experimental.pallas import tpu as pltpu
from jax.sharding import PartitionSpec as P

NX = 512
KY = 4
CLASSES = 2
ZBINS = 4
XBINS = 4
TAPS = 8
LANES = 128
QUARTERS = NX // LANES
PLANES = 32
CHUNKS = 4
UNROLL = 16
PARTS = 4
ROWS = QUARTERS * KY
PITCH = 2 * ROWS + 1
bf16, f32 = jnp.bfloat16, jnp.float32


def lanczos_taps(num_bins):
    fraction = (np.arange(num_bins, dtype=np.float32) + np.float32(0.5)) / np.float32(num_bins)
    distance = (np.arange(TAPS, dtype=np.float32) - np.float32(3.0))[None, :] - fraction[:, None]
    kernel = (np.sinc(distance) * np.sinc(distance / np.float32(4.0))).astype(np.float32)
    return (kernel / kernel.sum(-1, keepdims=True)).astype(jnp.bfloat16).astype(np.float32)


def turns_per_defocus():
    x = np.arange(NX)
    signed = (x + NX // 2) % NX - NX // 2
    y = np.arange(KY) + 1
    radius = 200.0 * (y[:, None] ** 2 + signed[None, :] ** 2) / NX**2
    table = radius.reshape(KY, QUARTERS, LANES).transpose(1, 0, 2).reshape(ROWS, LANES)
    return table.astype(np.float32)


def column_of(q):
    place = np.arange(LANES)
    quarter = (place - q) % QUARTERS
    return 4 * (LANES // QUARTERS * quarter + (place - q - quarter) % LANES // 4) + q


def fourier_table():
    out = np.zeros((QUARTERS, LANES, 2, LANES))
    for q in range(QUARTERS):
        wave = 2.0 * np.pi * ((np.arange(LANES)[:, None] * column_of(q)[None, :]) % NX) / NX
        out[q, :, 0], out[q, :, 1] = np.cos(wave), np.sin(wave)
    return out.reshape(QUARTERS, LANES, 2 * LANES).astype(jnp.bfloat16)


def factor_table(scale):
    taps = scale * lanczos_taps(XBINS).astype(np.float64)
    out = np.zeros((XBINS, QUARTERS, 2, LANES))
    for q in range(QUARTERS):
        shift = 2.0 * np.pi * (((np.arange(TAPS) - 3)[:, None] * column_of(q)[None, :]) % NX) / NX
        out[:, q, 0], out[:, q, 1] = taps @ np.cos(shift), taps @ np.sin(shift)
    return out.reshape(XBINS, 2 * NX).astype(np.float32)


def z_table(planes):
    z = np.arange(planes)
    angle = 2.0 * np.pi * ((z[:, None] * z[None, :]) % planes) / planes
    cos, sin = np.cos(angle), np.sin(angle)
    return np.stack([np.concatenate([cos, sin]), np.concatenate([-sin, cos])])


def sine_coefficients(terms=5):
    f = 0.5 * np.cos(np.linspace(0.0, np.pi / 2, 4001))
    basis = f[:, None] ** (2 * np.arange(terms) + 1)
    return np.linalg.lstsq(basis, np.sin(2 * np.pi * f), rcond=None)[0].astype(np.float32)


def slot_of(schedule, here, there):
    slots = [[row[at] for row in schedule].index(there) for at in range(4)]
    slot = jnp.int32(slots[0])
    for at in range(1, 4):
        slot = jnp.where(here == at, slots[at], slot)
    return slot


def quarter_sums(parts):
    (r0, i0), (r1, i1), (r2, i2), (r3, i3) = parts
    ar, ai, br, bi = r0 + r2, i0 + i2, r0 - r2, i0 - i2
    cr, ci, dr, di = r1 + r3, i1 + i3, r1 - r3, i1 - i3
    return (ar + cr, ai + ci), (br - di, bi + dr), (ar - cr, ai - ci), (br + di, bi - dr)


def transform(w_ref, half, ky_low, spread_ref, table_ref, factor_ref, v_ref, put):
    number = spread_ref.shape[1] // 2
    count = number // PARTS
    for at in range(0, number, count):
        sums = []
        for y in range(2):

            def column(r, p):
                row = p * KY + ky_low if p < 2 else jnp.where(half, (p - 2) * KY + 1 - ky_low, p * KY + ky_low)
                return w_ref[pl.ds(at * PITCH + r * ROWS + 2 * y + row, count, stride=PITCH), :]

            sums.append(quarter_sums([(column(0, p), column(1, p)) for p in range(QUARTERS)]))
        for q in range(QUARTERS):
            rows = jnp.concatenate([sums[y][q][r] for r in range(2) for y in range(2)], axis=0).astype(bf16)
            both = jnp.dot(rows, table_ref[q], preferred_element_type=f32)
            real = both[: 2 * count, :LANES] - both[2 * count :, LANES:]
            imag = both[: 2 * count, LANES:] + both[2 * count :, :LANES]
            by_real, by_imag = (
                factor_ref[at : at + count, (2 * q + s) * LANES : (2 * q + s + 1) * LANES] for s in range(2)
            )
            for y in range(2):
                part = slice(y * count, (y + 1) * count)
                to = slice((y * QUARTERS + q) * LANES, (y * QUARTERS + q + 1) * LANES)
                v_ref[at : at + count, to] = (real[part] * by_real - imag[part] * by_imag).astype(bf16)
                v_ref[number + at : number + at + count, to] = (
                    real[part] * by_imag + imag[part] * by_real
                ).astype(bf16)
    group = lax.broadcasted_iota(jnp.int32, (CLASSES * 2 * PLANES, LANES), 1) % QUARTERS
    for y in range(2):
        part = jnp.dot(spread_ref[...], v_ref[:, y * NX : (y + 1) * NX], preferred_element_type=f32)
        parts = [part[:, q * LANES : (q + 1) * LANES] for q in range(QUARTERS)]
        for quarter in range(QUARTERS):
            value = parts[-quarter % QUARTERS]
            for j in range(1, QUARTERS):
                value = jnp.where(group == j, parts[(j - quarter) % QUARTERS], value)
            value = value.astype(bf16)
            for cls in range(CLASSES):
                put(y, cls, quarter, value[cls * 2 * PLANES : (cls + 1) * 2 * PLANES])


def spread_matrix(pose, label, planes, first_plane):
    per_pose = ZBINS * XBINS
    taps = lanczos_taps(ZBINS)
    start, zbin = pose // per_pose, pose // XBINS % ZBINS
    shape = (CLASSES * PLANES, pose.shape[1])
    row = lax.broadcasted_iota(jnp.int32, shape, 0)
    tap = (first_plane + row % PLANES - start + planes) % planes
    tap = jnp.where(row // PLANES == label, tap, -1)
    out = jnp.zeros(shape, f32)
    for t in range(TAPS):
        weight = jnp.full(pose.shape, float(taps[0, t]), f32)
        for z in range(1, ZBINS):
            weight = jnp.where(zbin == z, float(taps[z, t]), weight)
        out = jnp.where(tap == t, weight, out)
    return out.astype(bf16)


def place(out_ref, core):
    slab, img = lax.axis_index("slab"), lax.axis_index("img")
    here, plane = slab % 2 * 2 + img // 2, slab // 2
    first = [
        jnp.where(core == 0, slot_of(FIRST[0], here, there), slot_of(FIRST[1], here, there)) for there in range(4)
    ]
    second = {
        schedule: [slot_of(schedule, plane, there) for there in range(4)] for schedule in dict.fromkeys(SECOND)
    }

    def put(y, cls, quarter, value):
        there = quarter % 2 * 2 + y
        out_ref[first[there] * 4 + second[SECOND[there]][cls * 2 + quarter // 2]] = value

    return put


def contrast(turns, focus):
    coefficients = [float(v) for v in sine_coefficients()]
    angle = turns * focus + 0.1 / (2 * math.pi)
    f = angle - jnp.round(angle)
    square = f * f
    poly = coefficients[-1] * square + coefficients[-2]
    for coefficient in coefficients[-3::-1]:
        poly = poly * square + coefficient
    return poly * f


def weigher(turns_ref, wide_ref, x_ref, w_ref):
    turns = turns_ref[...]

    def weigh(i, carry):
        ctf = contrast(turns, wide_ref[pl.ds(i, 1), :])
        rows = x_ref[pl.ds(pl.multiple_of(i * 2 * ROWS, 2 * ROWS), 2 * ROWS), :].astype(f32)
        w_ref[pl.ds(i * PITCH, ROWS), :] = ctf * rows[:ROWS]
        w_ref[pl.ds(i * PITCH + ROWS, ROWS), :] = ctf * rows[ROWS:]
        return carry

    return weigh


def half_weigher(ky_low, turns_ref, wide_ref, x_ref, w_ref):
    stays = lax.broadcasted_iota(jnp.int32, (8, LANES), 0) % 2 == ky_low
    shift = 1 if ky_low == 0 else 7

    def wanted(first, second):
        return jnp.where(stays, first, pltpu.roll(second, shift, 0))

    turns = wanted(turns_ref[0:8, :], turns_ref[8:16, :])

    def weigh(i, carry):
        ctf = contrast(turns, wide_ref[pl.ds(i, 1), :])
        rows = x_ref[pl.ds(pl.multiple_of(i * 2 * ROWS, 2 * ROWS), 2 * ROWS), :].astype(f32)
        w_ref[pl.ds(i * PITCH, 8), :] = ctf * wanted(rows[0:8], rows[8:16])
        w_ref[pl.ds(i * PITCH + ROWS, 8), :] = ctf * wanted(rows[16:24], rows[24:32])
        return carry

    return weigh


def first_kernel(planes, x_hbm, focus_hbm, pose_hbm, label_hbm, turns_hbm, bins_hbm, along_z_hbm, table_hbm,
                 out_ref, w_ref, x_ref, wide_ref, turns_ref, spread_ref, table_ref, factor_ref,
                 focus_ref, pose_ref, label_ref, bins_ref, along_z_ref, v_ref, sems):
    number = wide_ref.shape[0]
    chunk = x_ref.shape[0] // CHUNKS

    def copy(source, target, at):
        made = pltpu.make_async_copy(source, target, sems.at[at])
        made.start()
        return made

    small = [
        copy(source, target, at)
        for at, (source, target) in enumerate(
            (
                (focus_hbm, focus_ref),
                (turns_hbm, turns_ref),
                (pose_hbm, pose_ref),
                (label_hbm, label_ref),
                (bins_hbm, bins_ref),
                (along_z_hbm, along_z_ref),
            )
        )
    ]
    parts = [
        copy(x_hbm.at[pl.ds(c * chunk, chunk)], x_ref.at[pl.ds(c * chunk, chunk)], 6 + c) for c in range(CHUNKS)
    ]
    table = copy(table_hbm, table_ref, 6 + CHUNKS)
    for made in small:
        made.wait()
    core = lax.axis_index("img") % 2
    wide_ref[...] = jnp.broadcast_to(focus_ref[...].astype(f32), (LANES, number)).T
    planar = spread_matrix(pose_ref[...], label_ref[...], planes, 0)
    xbin = jnp.broadcast_to((pose_ref[...] % XBINS).astype(f32), (LANES, number)).T
    for at in range(0, 2 * NX, LANES):
        chosen = bins_ref[0:1, at : at + LANES]
        for b in range(1, XBINS):
            chosen = jnp.where(xbin == b, bins_ref[b : b + 1, at : at + LANES], chosen)
        factor_ref[:, at : at + LANES] = chosen
    full, half = weigher(turns_ref, wide_ref, x_ref, w_ref), half_weigher(1, turns_ref, wide_ref, x_ref, w_ref)
    for c in range(CHUNKS):
        parts[c].wait()
        first, last = c * number // CHUNKS, (c + 1) * number // CHUNKS

        @pl.when(core == 0)
        def _():
            lax.fori_loop(first, last, half, 0, unroll=UNROLL)

        @pl.when(core == 1)
        def _():
            lax.fori_loop(first, last, full, 0, unroll=UNROLL)

    table.wait()
    for s in range(2):
        spread = jnp.dot(along_z_ref[s], planar, preferred_element_type=f32).astype(bf16)
        spread_ref[:, s * number : (s + 1) * number] = spread
    transform(w_ref, core == 0, 1 - core, spread_ref, table_ref, factor_ref, v_ref, place(out_ref, 1 - core))


def second_kernel(w_in, x_ref, wide_ref, turns_ref, spread_ref, table_ref, factor_ref, out_ref, w_ref, v_ref):
    core = lax.axis_index("img") % 2

    @pl.when(core == 0)
    def _():
        half = half_weigher(0, turns_ref, wide_ref, x_ref, w_ref)
        lax.fori_loop(0, wide_ref.shape[0], half, 0, unroll=UNROLL)

    transform(w_ref, core == 0, core, spread_ref, table_ref, factor_ref, v_ref, place(out_ref, core))


def last_kernel(*refs):
    *got_refs, out_ref = refs
    quarter = lax.axis_index("slab") % QUARTERS
    total = sum(got_ref[...].astype(f32) for got_ref in got_refs)
    out_ref[...] = pltpu.roll(total, (LANES - quarter) % LANES, 1)


VMEM = pl.BlockSpec(memory_space=pltpu.VMEM)
SMEM = pl.BlockSpec(memory_space=pltpu.SMEM)
HBM = pl.BlockSpec(memory_space=pltpu.HBM)


FIRST = (((1, 0, 2, 3), (2, 3, 1, 0), (3, 2, 0, 1), (0, 1, 3, 2)),) * 2
USUAL = ((1, 2, 0, 3), (2, 1, 3, 0), (3, 0, 2, 1), (0, 3, 1, 2))
SECOND = (((1, 3, 2, 0), (2, 1, 0, 3), (3, 0, 1, 2), (0, 2, 3, 1)), USUAL, USUAL, USUAL)
FIRST_LISTED = (0, 3, 2, 1)
SECOND_LISTED = (3, 2, 1, 0)


def pairs_of(stage, slot):
    pairs = []
    for source in range(32):
        core, y, x, z = source & 1, source >> 1 & 1, source >> 2 & 1, source >> 3
        if stage == 0:
            to = FIRST[core][slot][2 * x + y]
            x, y = to >> 1, to & 1
        else:
            z = SECOND[2 * x + y][slot][z]
        pairs.append((source, z << 3 | x << 2 | y << 1 | 1 - core))
    return pairs


def ctf_weights(defocus):
    x_index = jnp.arange(NX, dtype=jnp.int32)
    signed = (x_index + NX // 2) % NX - NX // 2
    y_index = jnp.arange(KY, dtype=jnp.int32) + 1
    radius = (y_index[:, None] ** 2 + signed[None, :] ** 2).astype(f32) / float(NX * NX)
    phase = 400.0 * math.pi * defocus.astype(f32)[:, None, None] * radius[None]
    return jnp.sin(phase + 0.1)


def many_planes(images, pose_bins, labels, defocus):
    owners, groups = lax.axis_size("slab"), lax.axis_size("img")
    number = images.shape[0]
    planes = owners * 4
    weighted = (ctf_weights(defocus)[:, None] * images.astype(f32)).astype(bf16)
    table = jnp.asarray(fourier_table()).reshape(QUARTERS, LANES, 2, LANES)
    scale = 2.5 / math.sqrt(number * owners * groups * NX)
    factors = jnp.asarray(factor_table(scale)).reshape(XBINS, QUARTERS, 2, LANES)[pose_bins % XBINS]
    by_real, by_imag = (jnp.moveaxis(factors[:, :, s], 0, 1)[:, :, None] for s in range(2))
    quarters = jnp.moveaxis(weighted.astype(f32).reshape(number, 2, KY, QUARTERS, LANES), 3, 0)
    sums = quarter_sums([(part[:, 0], part[:, 1]) for part in quarters])
    sums = jnp.stack([jnp.stack(pair) for pair in sums]).astype(bf16)
    both = jnp.einsum("qrikm,qmsn->rsqikn", sums, table, preferred_element_type=f32)
    real, imag = both[0, 0] - both[1, 1], both[0, 1] + both[1, 0]
    turned = jnp.stack([real * by_real - imag * by_imag, real * by_imag + imag * by_real]).astype(bf16)
    columns = np.argsort(np.concatenate([column_of(q) for q in range(QUARTERS)]))
    turned = jnp.moveaxis(turned, 1, 3).reshape(2, number, KY, NX)[..., columns]

    def block(first_plane):
        spread = spread_matrix(pose_bins[None], labels[None], planes, first_plane)
        spread = spread.reshape(CLASSES, PLANES, number)
        return jnp.einsum("czi,sikx->kcxsz", spread, turned, preferred_element_type=f32).astype(bf16)

    parts = lax.map(block, jnp.arange(planes // PLANES, dtype=jnp.int32) * PLANES)
    parts = jnp.moveaxis(parts, 0, -2).reshape(KY, CLASSES * NX, 2, planes).astype(f32)
    total = lax.psum_scatter(parts, "img", scatter_dimension=0, tiled=True)
    total = lax.psum_scatter(total, "slab", scatter_dimension=1, tiled=True)
    table = jnp.asarray(z_table(planes).astype(np.float32)).reshape(2, 2, planes, planes)
    return jnp.einsum("yqsz,stwz->yqtw", total, table, precision=lax.Precision.HIGHEST)


def on_device(images, pose_bins, labels, defocus):
    owners, groups = lax.axis_size("slab"), lax.axis_size("img")
    number = images.shape[0]
    planes = owners * 4
    if planes != PLANES:
        return many_planes(images, pose_bins, labels, defocus)
    scale = 2.5 / math.sqrt(number * owners * groups * NX)
    x = images.reshape(number, 2, KY, QUARTERS, LANES).transpose(0, 1, 3, 2, 4).reshape(number * 2 * ROWS, LANES)
    pieces = 2 * CLASSES * QUARTERS
    w_shape = jax.ShapeDtypeStruct((number * PITCH + 40, LANES), f32)
    turns = jnp.asarray(turns_per_defocus())
    spread_shape = jax.ShapeDtypeStruct((CLASSES * 2 * PLANES, 2 * number), bf16)
    piece_shape = jax.ShapeDtypeStruct((pieces, 2 * PLANES, LANES), bf16)
    table = jnp.asarray(fourier_table())
    table_shape = jax.ShapeDtypeStruct(table.shape, bf16)
    bins = jnp.asarray(factor_table(scale))
    along_z = jnp.asarray(np.stack([np.kron(np.eye(CLASSES), part) for part in z_table(planes)]).astype(jnp.bfloat16))
    factor_shape = jax.ShapeDtypeStruct((number, 2 * NX), f32)
    work = [pltpu.VMEM((2 * number, 2 * NX), bf16)]
    other, *near = pl.pallas_call(
        functools.partial(first_kernel, planes),
        out_shape=(
            piece_shape,
            w_shape,
            jax.ShapeDtypeStruct(x.shape, bf16),
            jax.ShapeDtypeStruct((number, LANES), f32),
            jax.ShapeDtypeStruct(turns.shape, f32),
            spread_shape,
            table_shape,
            factor_shape,
        ),
        in_specs=[HBM] * 8,
        out_specs=(VMEM,) * 8,
        scratch_shapes=[
            pltpu.VMEM((1, number), bf16),
            pltpu.VMEM((1, number), jnp.int32),
            pltpu.VMEM((1, number), jnp.int32),
            pltpu.VMEM(bins.shape, f32),
            pltpu.VMEM(along_z.shape, bf16),
            *work,
            pltpu.SemaphoreType.DMA((CHUNKS + 7,)),
        ],
        compiler_params=pltpu.CompilerParams(vmem_limit_bytes=32 << 20),
        name="weigh_and_transform_other",
    )(*(
        pltpu.with_memory_space_constraint(v, pltpu.HBM)
        for v in (x, defocus[None], pose_bins[None], labels[None], turns, bins, along_z, table)
    ))
    axes = ("slab", "img")
    got = lax.ppermute(other, axes, [(i, i ^ 1) for i in range(owners * groups)])
    own, _ = pl.pallas_call(
        second_kernel,
        out_shape=(piece_shape, w_shape),
        in_specs=[VMEM] * 7,
        out_specs=(VMEM, VMEM),
        input_output_aliases={0: 1},
        scratch_shapes=work,
        compiler_params=pltpu.CompilerParams(vmem_limit_bytes=16 << 20),
        name="transform_own",
    )(*near)
    total = (own.astype(f32) + got.astype(f32)).astype(bf16)
    got = [lax.ppermute(total[4 * slot : 4 * slot + 4], axes, pairs_of(0, slot)) for slot in FIRST_LISTED]
    total = sum(g.astype(f32) for g in got).astype(bf16)
    got = [lax.ppermute(total[slot], axes, pairs_of(1, slot)) for slot in SECOND_LISTED]
    out = pl.pallas_call(
        last_kernel,
        out_shape=jax.ShapeDtypeStruct((2 * planes, LANES), f32),
        in_specs=[VMEM] * 4,
        out_specs=VMEM,
        compiler_params=pltpu.CompilerParams(vmem_limit_bytes=16 << 20),
        name="add_last",
    )(*got)
    return out.reshape(1, 2, planes, LANES).transpose(0, 3, 1, 2)


def solution(mesh):
    placed = (
        P(("slab", "img"), None, None, None),
        P(("slab", "img")),
        P(("slab", "img")),
        P(("slab", "img")),
    )
    return jax.shard_map(
        on_device, mesh=mesh, in_specs=placed, out_specs=P("img", "slab", None, None), check_vma=False
    )
```

```python
import functools
import math

import jax
import jax.numpy as jnp
import numpy as np
from jax import lax
from jax.experimental import pallas as pl
from jax.experimental.pallas import tpu as pltpu
from jax.sharding import PartitionSpec as P

NX = 512
KY = 4
CLASSES = 2
ZBINS = 4
XBINS = 4
TAPS = 8
LANES = 128
QUARTERS = NX // LANES
PLANES = 32
CHUNKS = 4
UNROLL = 16
PARTS = 4
ROWS = QUARTERS * KY
PITCH = 2 * ROWS + 1
bf16, f32 = jnp.bfloat16, jnp.float32


def lanczos_taps(num_bins):
    fraction = (np.arange(num_bins, dtype=np.float32) + np.float32(0.5)) / np.float32(num_bins)
    distance = (np.arange(TAPS, dtype=np.float32) - np.float32(3.0))[None, :] - fraction[:, None]
    kernel = (np.sinc(distance) * np.sinc(distance / np.float32(4.0))).astype(np.float32)
    return (kernel / kernel.sum(-1, keepdims=True)).astype(jnp.bfloat16).astype(np.float32)


def turns_per_defocus():
    x = np.arange(NX)
    signed = (x + NX // 2) % NX - NX // 2
    y = np.arange(KY) + 1
    radius = 200.0 * (y[:, None] ** 2 + signed[None, :] ** 2) / NX**2
    table = radius.reshape(KY, QUARTERS, LANES).transpose(1, 0, 2).reshape(ROWS, LANES)
    return table.astype(np.float32)


def column_of(q):
    place = np.arange(LANES)
    quarter = (place - q) % QUARTERS
    return 4 * (LANES // QUARTERS * quarter + (place - q - quarter) % LANES // 4) + q


def fourier_table():
    out = np.zeros((QUARTERS, LANES, 2, LANES))
    for q in range(QUARTERS):
        wave = 2.0 * np.pi * ((np.arange(LANES)[:, None] * column_of(q)[None, :]) % NX) / NX
        out[q, :, 0], out[q, :, 1] = np.cos(wave), np.sin(wave)
    return out.reshape(QUARTERS, LANES, 2 * LANES).astype(jnp.bfloat16)


def factor_table(scale):
    taps = scale * lanczos_taps(XBINS).astype(np.float64)
    out = np.zeros((XBINS, QUARTERS, 2, LANES))
    for q in range(QUARTERS):
        shift = 2.0 * np.pi * (((np.arange(TAPS) - 3)[:, None] * column_of(q)[None, :]) % NX) / NX
        out[:, q, 0], out[:, q, 1] = taps @ np.cos(shift), taps @ np.sin(shift)
    return out.reshape(XBINS, 2 * NX).astype(np.float32)


def z_table(planes):
    z = np.arange(planes)
    angle = 2.0 * np.pi * ((z[:, None] * z[None, :]) % planes) / planes
    cos, sin = np.cos(angle), np.sin(angle)
    return np.stack([np.concatenate([cos, sin]), np.concatenate([-sin, cos])])


def sine_coefficients(terms=5):
    f = 0.5 * np.cos(np.linspace(0.0, np.pi / 2, 4001))
    basis = f[:, None] ** (2 * np.arange(terms) + 1)
    return np.linalg.lstsq(basis, np.sin(2 * np.pi * f), rcond=None)[0].astype(np.float32)


def slot_of(schedule, here, there):
    slots = [[row[at] for row in schedule].index(there) for at in range(4)]
    slot = jnp.int32(slots[0])
    for at in range(1, 4):
        slot = jnp.where(here == at, slots[at], slot)
    return slot


def quarter_sums(parts):
    (r0, i0), (r1, i1), (r2, i2), (r3, i3) = parts
    ar, ai, br, bi = r0 + r2, i0 + i2, r0 - r2, i0 - i2
    cr, ci, dr, di = r1 + r3, i1 + i3, r1 - r3, i1 - i3
    return (ar + cr, ai + ci), (br - di, bi + dr), (ar - cr, ai - ci), (br + di, bi - dr)


def transform(w_ref, half, ky_low, spread_ref, table_ref, factor_ref, v_ref, put):
    number = spread_ref.shape[1] // 2
    count = number // PARTS
    for at in range(0, number, count):
        sums = []
        for y in range(2):

            def column(r, p):
                row = p * KY + ky_low if p < 2 else jnp.where(half, (p - 2) * KY + 1 - ky_low, p * KY + ky_low)
                return w_ref[pl.ds(at * PITCH + r * ROWS + 2 * y + row, count, stride=PITCH), :]

            sums.append(quarter_sums([(column(0, p), column(1, p)) for p in range(QUARTERS)]))
        for q in range(QUARTERS):
            rows = jnp.concatenate([sums[y][q][r] for r in range(2) for y in range(2)], axis=0).astype(bf16)
            both = jnp.dot(rows, table_ref[q], preferred_element_type=f32)
            real = both[: 2 * count, :LANES] - both[2 * count :, LANES:]
            imag = both[: 2 * count, LANES:] + both[2 * count :, :LANES]
            by_real, by_imag = (
                factor_ref[at : at + count, (2 * q + s) * LANES : (2 * q + s + 1) * LANES] for s in range(2)
            )
            for y in range(2):
                part = slice(y * count, (y + 1) * count)
                to = slice((y * QUARTERS + q) * LANES, (y * QUARTERS + q + 1) * LANES)
                v_ref[at : at + count, to] = (real[part] * by_real - imag[part] * by_imag).astype(bf16)
                v_ref[number + at : number + at + count, to] = (
                    real[part] * by_imag + imag[part] * by_real
                ).astype(bf16)
    group = lax.broadcasted_iota(jnp.int32, (CLASSES * 2 * PLANES, LANES), 1) % QUARTERS
    for y in range(2):
        part = jnp.dot(spread_ref[...], v_ref[:, y * NX : (y + 1) * NX], preferred_element_type=f32)
        parts = [part[:, q * LANES : (q + 1) * LANES] for q in range(QUARTERS)]
        for quarter in range(QUARTERS):
            value = parts[-quarter % QUARTERS]
            for j in range(1, QUARTERS):
                value = jnp.where(group == j, parts[(j - quarter) % QUARTERS], value)
            value = value.astype(bf16)
            for cls in range(CLASSES):
                put(y, cls, quarter, value[cls * 2 * PLANES : (cls + 1) * 2 * PLANES])


def spread_matrix(pose, label, planes, first_plane):
    per_pose = ZBINS * XBINS
    taps = lanczos_taps(ZBINS)
    start, zbin = pose // per_pose, pose // XBINS % ZBINS
    shape = (CLASSES * PLANES, pose.shape[1])
    row = lax.broadcasted_iota(jnp.int32, shape, 0)
    tap = (first_plane + row % PLANES - start + planes) % planes
    tap = jnp.where(row // PLANES == label, tap, -1)
    out = jnp.zeros(shape, f32)
    for t in range(TAPS):
        weight = jnp.full(pose.shape, float(taps[0, t]), f32)
        for z in range(1, ZBINS):
            weight = jnp.where(zbin == z, float(taps[z, t]), weight)
        out = jnp.where(tap == t, weight, out)
    return out.astype(bf16)


def place(out_ref, core):
    slab, img = lax.axis_index("slab"), lax.axis_index("img")
    here, plane = slab % 2 * 2 + img // 2, slab // 2
    first = [
        jnp.where(core == 0, slot_of(FIRST[0], here, there), slot_of(FIRST[1], here, there)) for there in range(4)
    ]
    second = {
        schedule: [slot_of(schedule, plane, there) for there in range(4)] for schedule in dict.fromkeys(SECOND)
    }

    def put(y, cls, quarter, value):
        there = quarter % 2 * 2 + y
        out_ref[first[there] * 4 + second[SECOND[there]][cls * 2 + quarter // 2]] = value

    return put


def contrast(turns, focus):
    coefficients = [float(v) for v in sine_coefficients()]
    angle = turns * focus + 0.1 / (2 * math.pi)
    f = angle - jnp.round(angle)
    square = f * f
    poly = coefficients[-1] * square + coefficients[-2]
    for coefficient in coefficients[-3::-1]:
        poly = poly * square + coefficient
    return poly * f


def weigher(turns_ref, wide_ref, x_ref, w_ref):
    turns = turns_ref[...]

    def weigh(i, carry):
        ctf = contrast(turns, wide_ref[pl.ds(i, 1), :])
        rows = x_ref[pl.ds(pl.multiple_of(i * 2 * ROWS, 2 * ROWS), 2 * ROWS), :].astype(f32)
        w_ref[pl.ds(i * PITCH, ROWS), :] = ctf * rows[:ROWS]
        w_ref[pl.ds(i * PITCH + ROWS, ROWS), :] = ctf * rows[ROWS:]
        return carry

    return weigh


def half_weigher(ky_low, turns_ref, wide_ref, x_ref, w_ref):
    stays = lax.broadcasted_iota(jnp.int32, (8, LANES), 0) % 2 == ky_low
    shift = 1 if ky_low == 0 else 7

    def wanted(first, second):
        return jnp.where(stays, first, pltpu.roll(second, shift, 0))

    turns = wanted(turns_ref[0:8, :], turns_ref[8:16, :])

    def weigh(i, carry):
        ctf = contrast(turns, wide_ref[pl.ds(i, 1), :])
        rows = x_ref[pl.ds(pl.multiple_of(i * 2 * ROWS, 2 * ROWS), 2 * ROWS), :].astype(f32)
        w_ref[pl.ds(i * PITCH, 8), :] = ctf * wanted(rows[0:8], rows[8:16])
        w_ref[pl.ds(i * PITCH + ROWS, 8), :] = ctf * wanted(rows[16:24], rows[24:32])
        return carry

    return weigh


def first_kernel(planes, x_hbm, focus_hbm, pose_hbm, label_hbm, turns_hbm, bins_hbm, along_z_hbm, table_hbm,
                 out_ref, w_ref, x_ref, wide_ref, turns_ref, spread_ref, table_ref, factor_ref,
                 focus_ref, pose_ref, label_ref, bins_ref, along_z_ref, v_ref, sems):
    number = wide_ref.shape[0]
    chunk = x_ref.shape[0] // CHUNKS

    def copy(source, target, at):
        made = pltpu.make_async_copy(source, target, sems.at[at])
        made.start()
        return made

    small = [
        copy(source, target, at)
        for at, (source, target) in enumerate(
            (
                (focus_hbm, focus_ref),
                (turns_hbm, turns_ref),
                (pose_hbm, pose_ref),
                (label_hbm, label_ref),
                (bins_hbm, bins_ref),
                (along_z_hbm, along_z_ref),
            )
        )
    ]
    parts = [
        copy(x_hbm.at[pl.ds(c * chunk, chunk)], x_ref.at[pl.ds(c * chunk, chunk)], 6 + c) for c in range(CHUNKS)
    ]
    table = copy(table_hbm, table_ref, 6 + CHUNKS)
    for made in small:
        made.wait()
    core = lax.axis_index("img") % 2
    wide_ref[...] = jnp.broadcast_to(focus_ref[...].astype(f32), (LANES, number)).T
    planar = spread_matrix(pose_ref[...], label_ref[...], planes, 0)
    xbin = jnp.broadcast_to((pose_ref[...] % XBINS).astype(f32), (LANES, number)).T
    for at in range(0, 2 * NX, LANES):
        chosen = bins_ref[0:1, at : at + LANES]
        for b in range(1, XBINS):
            chosen = jnp.where(xbin == b, bins_ref[b : b + 1, at : at + LANES], chosen)
        factor_ref[:, at : at + LANES] = chosen
    full, half = weigher(turns_ref, wide_ref, x_ref, w_ref), half_weigher(1, turns_ref, wide_ref, x_ref, w_ref)
    for c in range(CHUNKS):
        parts[c].wait()
        first, last = c * number // CHUNKS, (c + 1) * number // CHUNKS

        @pl.when(core == 0)
        def _():
            lax.fori_loop(first, last, half, 0, unroll=UNROLL)

        @pl.when(core == 1)
        def _():
            lax.fori_loop(first, last, full, 0, unroll=UNROLL)

    table.wait()
    for s in range(2):
        spread = jnp.dot(along_z_ref[s], planar, preferred_element_type=f32).astype(bf16)
        spread_ref[:, s * number : (s + 1) * number] = spread
    transform(w_ref, core == 0, 1 - core, spread_ref, table_ref, factor_ref, v_ref, place(out_ref, 1 - core))


def second_kernel(w_in, x_ref, wide_ref, turns_ref, spread_ref, table_ref, factor_ref, out_ref, w_ref, v_ref):
    core = lax.axis_index("img") % 2

    @pl.when(core == 0)
    def _():
        half = half_weigher(0, turns_ref, wide_ref, x_ref, w_ref)
        lax.fori_loop(0, wide_ref.shape[0], half, 0, unroll=UNROLL)

    transform(w_ref, core == 0, core, spread_ref, table_ref, factor_ref, v_ref, place(out_ref, core))


def last_kernel(*refs):
    *got_refs, out_ref = refs
    quarter = lax.axis_index("slab") % QUARTERS
    total = sum(got_ref[...].astype(f32) for got_ref in got_refs)
    out_ref[...] = pltpu.roll(total, (LANES - quarter) % LANES, 1)


VMEM = pl.BlockSpec(memory_space=pltpu.VMEM)
SMEM = pl.BlockSpec(memory_space=pltpu.SMEM)
HBM = pl.BlockSpec(memory_space=pltpu.HBM)


FIRST = (
    ((2, 1, 0, 3), (1, 2, 3, 0), (3, 0, 2, 1), (0, 3, 1, 2)),
    ((1, 0, 2, 3), (2, 3, 1, 0), (3, 1, 0, 2), (0, 2, 3, 1)),
)
USUAL = ((1, 2, 0, 3), (2, 1, 3, 0), (3, 0, 2, 1), (0, 3, 1, 2))
SECOND = (((1, 3, 2, 0), (2, 1, 0, 3), (3, 0, 1, 2), (0, 2, 3, 1)), USUAL, USUAL, USUAL)
FIRST_LISTED = (0, 3, 2, 1)
SECOND_LISTED = (3, 2, 1, 0)


def pairs_of(stage, slot):
    pairs = []
    for source in range(32):
        core, y, x, z = source & 1, source >> 1 & 1, source >> 2 & 1, source >> 3
        if stage == 0:
            to = FIRST[core][slot][2 * x + y]
            x, y = to >> 1, to & 1
        else:
            z = SECOND[2 * x + y][slot][z]
        pairs.append((source, z << 3 | x << 2 | y << 1 | 1 - core))
    return pairs


def ctf_weights(defocus):
    x_index = jnp.arange(NX, dtype=jnp.int32)
    signed = (x_index + NX // 2) % NX - NX // 2
    y_index = jnp.arange(KY, dtype=jnp.int32) + 1
    radius = (y_index[:, None] ** 2 + signed[None, :] ** 2).astype(f32) / float(NX * NX)
    phase = 400.0 * math.pi * defocus.astype(f32)[:, None, None] * radius[None]
    return jnp.sin(phase + 0.1)


def many_planes(images, pose_bins, labels, defocus):
    owners, groups = lax.axis_size("slab"), lax.axis_size("img")
    number = images.shape[0]
    planes = owners * 4
    weighted = (ctf_weights(defocus)[:, None] * images.astype(f32)).astype(bf16)
    table = jnp.asarray(fourier_table()).reshape(QUARTERS, LANES, 2, LANES)
    scale = 2.5 / math.sqrt(number * owners * groups * NX)
    factors = jnp.asarray(factor_table(scale)).reshape(XBINS, QUARTERS, 2, LANES)[pose_bins % XBINS]
    by_real, by_imag = (jnp.moveaxis(factors[:, :, s], 0, 1)[:, :, None] for s in range(2))
    quarters = jnp.moveaxis(weighted.astype(f32).reshape(number, 2, KY, QUARTERS, LANES), 3, 0)
    sums = quarter_sums([(part[:, 0], part[:, 1]) for part in quarters])
    sums = jnp.stack([jnp.stack(pair) for pair in sums]).astype(bf16)
    both = jnp.einsum("qrikm,qmsn->rsqikn", sums, table, preferred_element_type=f32)
    real, imag = both[0, 0] - both[1, 1], both[0, 1] + both[1, 0]
    turned = jnp.stack([real * by_real - imag * by_imag, real * by_imag + imag * by_real]).astype(bf16)
    columns = np.argsort(np.concatenate([column_of(q) for q in range(QUARTERS)]))
    turned = jnp.moveaxis(turned, 1, 3).reshape(2, number, KY, NX)[..., columns]

    def block(first_plane):
        spread = spread_matrix(pose_bins[None], labels[None], planes, first_plane)
        spread = spread.reshape(CLASSES, PLANES, number)
        return jnp.einsum("czi,sikx->kcxsz", spread, turned, preferred_element_type=f32).astype(bf16)

    parts = lax.map(block, jnp.arange(planes // PLANES, dtype=jnp.int32) * PLANES)
    parts = jnp.moveaxis(parts, 0, -2).reshape(KY, CLASSES * NX, 2, planes).astype(f32)
    total = lax.psum_scatter(parts, "img", scatter_dimension=0, tiled=True)
    total = lax.psum_scatter(total, "slab", scatter_dimension=1, tiled=True)
    table = jnp.asarray(z_table(planes).astype(np.float32)).reshape(2, 2, planes, planes)
    return jnp.einsum("yqsz,stwz->yqtw", total, table, precision=lax.Precision.HIGHEST)


def on_device(images, pose_bins, labels, defocus):
    owners, groups = lax.axis_size("slab"), lax.axis_size("img")
    number = images.shape[0]
    planes = owners * 4
    if planes != PLANES:
        return many_planes(images, pose_bins, labels, defocus)
    scale = 2.5 / math.sqrt(number * owners * groups * NX)
    x = images.reshape(number, 2, KY, QUARTERS, LANES).transpose(0, 1, 3, 2, 4).reshape(number * 2 * ROWS, LANES)
    pieces = 2 * CLASSES * QUARTERS
    w_shape = jax.ShapeDtypeStruct((number * PITCH + 40, LANES), f32)
    turns = jnp.asarray(turns_per_defocus())
    spread_shape = jax.ShapeDtypeStruct((CLASSES * 2 * PLANES, 2 * number), bf16)
    piece_shape = jax.ShapeDtypeStruct((pieces, 2 * PLANES, LANES), bf16)
    table = jnp.asarray(fourier_table())
    table_shape = jax.ShapeDtypeStruct(table.shape, bf16)
    bins = jnp.asarray(factor_table(scale))
    along_z = jnp.asarray(np.stack([np.kron(np.eye(CLASSES), part) for part in z_table(planes)]).astype(jnp.bfloat16))
    factor_shape = jax.ShapeDtypeStruct((number, 2 * NX), f32)
    work = [pltpu.VMEM((2 * number, 2 * NX), bf16)]
    other, *near = pl.pallas_call(
        functools.partial(first_kernel, planes),
        out_shape=(
            piece_shape,
            w_shape,
            jax.ShapeDtypeStruct(x.shape, bf16),
            jax.ShapeDtypeStruct((number, LANES), f32),
            jax.ShapeDtypeStruct(turns.shape, f32),
            spread_shape,
            table_shape,
            factor_shape,
        ),
        in_specs=[HBM] * 8,
        out_specs=(VMEM,) * 8,
        scratch_shapes=[
            pltpu.VMEM((1, number), bf16),
            pltpu.VMEM((1, number), jnp.int32),
            pltpu.VMEM((1, number), jnp.int32),
            pltpu.VMEM(bins.shape, f32),
            pltpu.VMEM(along_z.shape, bf16),
            *work,
            pltpu.SemaphoreType.DMA((CHUNKS + 7,)),
        ],
        compiler_params=pltpu.CompilerParams(vmem_limit_bytes=32 << 20),
        name="weigh_and_transform_other",
    )(*(
        pltpu.with_memory_space_constraint(v, pltpu.HBM)
        for v in (x, defocus[None], pose_bins[None], labels[None], turns, bins, along_z, table)
    ))
    axes = ("slab", "img")
    got = lax.ppermute(other, axes, [(i, i ^ 1) for i in range(owners * groups)])
    own, _ = pl.pallas_call(
        second_kernel,
        out_shape=(piece_shape, w_shape),
        in_specs=[VMEM] * 7,
        out_specs=(VMEM, VMEM),
        input_output_aliases={0: 1},
        scratch_shapes=work,
        compiler_params=pltpu.CompilerParams(vmem_limit_bytes=16 << 20),
        name="transform_own",
    )(*near)
    total = (own.astype(f32) + got.astype(f32)).astype(bf16)
    got = [lax.ppermute(total[4 * slot : 4 * slot + 4], axes, pairs_of(0, slot)) for slot in FIRST_LISTED]
    total = sum(g.astype(f32) for g in got).astype(bf16)
    got = [lax.ppermute(total[slot], axes, pairs_of(1, slot)) for slot in SECOND_LISTED]
    out = pl.pallas_call(
        last_kernel,
        out_shape=jax.ShapeDtypeStruct((2 * planes, LANES), f32),
        in_specs=[VMEM] * 4,
        out_specs=VMEM,
        compiler_params=pltpu.CompilerParams(vmem_limit_bytes=16 << 20),
        name="add_last",
    )(*got)
    return out.reshape(1, 2, planes, LANES).transpose(0, 3, 1, 2)


def solution(mesh):
    placed = (
        P(("slab", "img"), None, None, None),
        P(("slab", "img")),
        P(("slab", "img")),
        P(("slab", "img")),
    )
    return jax.shard_map(
        on_device, mesh=mesh, in_specs=placed, out_specs=P("img", "slab", None, None), check_vma=False
    )
```

```python
import functools
import math

import jax
import jax.numpy as jnp
import numpy as np
from jax import lax
from jax.experimental import pallas as pl
from jax.experimental.pallas import tpu as pltpu
from jax.sharding import PartitionSpec as P

NX = 512
KY = 4
CLASSES = 2
ZBINS = 4
XBINS = 4
TAPS = 8
LANES = 128
QUARTERS = NX // LANES
PLANES = 32
CHUNKS = 4
UNROLL = 32
PARTS = 4
ROWS = QUARTERS * KY
PITCH = 2 * ROWS + 1
bf16, f32 = jnp.bfloat16, jnp.float32


def lanczos_taps(num_bins):
    fraction = (np.arange(num_bins, dtype=np.float32) + np.float32(0.5)) / np.float32(num_bins)
    distance = (np.arange(TAPS, dtype=np.float32) - np.float32(3.0))[None, :] - fraction[:, None]
    kernel = (np.sinc(distance) * np.sinc(distance / np.float32(4.0))).astype(np.float32)
    return (kernel / kernel.sum(-1, keepdims=True)).astype(jnp.bfloat16).astype(np.float32)


def turns_per_defocus():
    x = np.arange(NX)
    signed = (x + NX // 2) % NX - NX // 2
    y = np.arange(KY) + 1
    radius = 200.0 * (y[:, None] ** 2 + signed[None, :] ** 2) / NX**2
    table = radius.reshape(KY, QUARTERS, LANES).transpose(1, 0, 2).reshape(ROWS, LANES)
    return table.astype(np.float32)


def column_of(q):
    place = np.arange(LANES)
    quarter = (place - q) % QUARTERS
    return 4 * (LANES // QUARTERS * quarter + (place - q - quarter) % LANES // 4) + q


def fourier_table():
    out = np.zeros((QUARTERS, LANES, 2, LANES))
    for q in range(QUARTERS):
        wave = 2.0 * np.pi * ((np.arange(LANES)[:, None] * column_of(q)[None, :]) % NX) / NX
        out[q, :, 0], out[q, :, 1] = np.cos(wave), np.sin(wave)
    return out.reshape(QUARTERS, LANES, 2 * LANES).astype(jnp.bfloat16)


def factor_table(scale):
    taps = scale * lanczos_taps(XBINS).astype(np.float64)
    out = np.zeros((XBINS, QUARTERS, 2, LANES))
    for q in range(QUARTERS):
        shift = 2.0 * np.pi * (((np.arange(TAPS) - 3)[:, None] * column_of(q)[None, :]) % NX) / NX
        out[:, q, 0], out[:, q, 1] = taps @ np.cos(shift), taps @ np.sin(shift)
    return out.reshape(XBINS, 2 * NX).astype(np.float32)


def z_table(planes):
    z = np.arange(planes)
    angle = 2.0 * np.pi * ((z[:, None] * z[None, :]) % planes) / planes
    cos, sin = np.cos(angle), np.sin(angle)
    return np.stack([np.concatenate([cos, sin]), np.concatenate([-sin, cos])])


def sine_coefficients(terms=5):
    f = 0.5 * np.cos(np.linspace(0.0, np.pi / 2, 4001))
    basis = f[:, None] ** (2 * np.arange(terms) + 1)
    return np.linalg.lstsq(basis, np.sin(2 * np.pi * f), rcond=None)[0].astype(np.float32)


def slot_of(schedule, here, there):
    slots = [[row[at] for row in schedule].index(there) for at in range(4)]
    slot = jnp.int32(slots[0])
    for at in range(1, 4):
        slot = jnp.where(here == at, slots[at], slot)
    return slot


def quarter_sums(parts):
    (r0, i0), (r1, i1), (r2, i2), (r3, i3) = parts
    ar, ai, br, bi = r0 + r2, i0 + i2, r0 - r2, i0 - i2
    cr, ci, dr, di = r1 + r3, i1 + i3, r1 - r3, i1 - i3
    return (ar + cr, ai + ci), (br - di, bi + dr), (ar - cr, ai - ci), (br + di, bi - dr)


def transform(w_ref, half, ky_low, spread_ref, table_ref, factor_ref, v_ref, put):
    number = spread_ref.shape[1] // 2
    count = number // PARTS
    for at in range(0, number, count):
        sums = []
        for y in range(2):

            def column(r, p):
                row = p * KY + ky_low if p < 2 else jnp.where(half, (p - 2) * KY + 1 - ky_low, p * KY + ky_low)
                return w_ref[pl.ds(at * PITCH + r * ROWS + 2 * y + row, count, stride=PITCH), :]

            sums.append(quarter_sums([(column(0, p), column(1, p)) for p in range(QUARTERS)]))
        for q in range(QUARTERS):
            rows = jnp.concatenate([sums[y][q][r] for r in range(2) for y in range(2)], axis=0).astype(bf16)
            both = jnp.dot(rows, table_ref[q], preferred_element_type=f32)
            real = both[: 2 * count, :LANES] - both[2 * count :, LANES:]
            imag = both[: 2 * count, LANES:] + both[2 * count :, :LANES]
            by_real, by_imag = (
                factor_ref[at : at + count, (2 * q + s) * LANES : (2 * q + s + 1) * LANES] for s in range(2)
            )
            for y in range(2):
                part = slice(y * count, (y + 1) * count)
                to = slice((y * QUARTERS + q) * LANES, (y * QUARTERS + q + 1) * LANES)
                v_ref[at : at + count, to] = (real[part] * by_real - imag[part] * by_imag).astype(bf16)
                v_ref[number + at : number + at + count, to] = (
                    real[part] * by_imag + imag[part] * by_real
                ).astype(bf16)
    group = lax.broadcasted_iota(jnp.int32, (CLASSES * 2 * PLANES, LANES), 1) % QUARTERS
    for y in range(2):
        part = jnp.dot(spread_ref[...], v_ref[:, y * NX : (y + 1) * NX], preferred_element_type=f32)
        parts = [part[:, q * LANES : (q + 1) * LANES] for q in range(QUARTERS)]
        for quarter in range(QUARTERS):
            value = parts[-quarter % QUARTERS]
            for j in range(1, QUARTERS):
                value = jnp.where(group == j, parts[(j - quarter) % QUARTERS], value)
            if quarter:
                value = pltpu.roll(value, LANES - quarter, 1)
            value = value.astype(bf16)
            for cls in range(CLASSES):
                put(y, cls, quarter, value[cls * 2 * PLANES : (cls + 1) * 2 * PLANES])


def spread_matrix(pose, label, planes, first_plane):
    per_pose = ZBINS * XBINS
    taps = lanczos_taps(ZBINS)
    start, zbin = pose // per_pose, pose // XBINS % ZBINS
    shape = (CLASSES * PLANES, pose.shape[1])
    row = lax.broadcasted_iota(jnp.int32, shape, 0)
    tap = (first_plane + row % PLANES - start + planes) % planes
    tap = jnp.where(row // PLANES == label, tap, -1)
    out = jnp.zeros(shape, f32)
    for t in range(TAPS):
        weight = jnp.full(pose.shape, float(taps[0, t]), f32)
        for z in range(1, ZBINS):
            weight = jnp.where(zbin == z, float(taps[z, t]), weight)
        out = jnp.where(tap == t, weight, out)
    return out.astype(bf16)


def place(out_ref, core):
    slab, img = lax.axis_index("slab"), lax.axis_index("img")
    here, plane = slab % 2 * 2 + img // 2, slab // 2
    first = [
        jnp.where(core == 0, slot_of(FIRST[0], here, there), slot_of(FIRST[1], here, there)) for there in range(4)
    ]
    second = {
        schedule: [slot_of(schedule, plane, there) for there in range(4)] for schedule in dict.fromkeys(SECOND)
    }

    def put(y, cls, quarter, value):
        there = quarter % 2 * 2 + y
        out_ref[first[there] * 4 + second[SECOND[there]][cls * 2 + quarter // 2]] = value

    return put


def contrast(turns, focus):
    coefficients = [float(v) for v in sine_coefficients()]
    angle = turns * focus + 0.1 / (2 * math.pi)
    f = angle - jnp.round(angle)
    square = f * f
    poly = coefficients[-1] * square + coefficients[-2]
    for coefficient in coefficients[-3::-1]:
        poly = poly * square + coefficient
    return poly * f


def weigher(turns_ref, wide_ref, x_ref, w_ref):
    turns = turns_ref[...]

    def weigh(i, carry):
        ctf = contrast(turns, wide_ref[pl.ds(i, 1), :])
        rows = x_ref[pl.ds(pl.multiple_of(i * 2 * ROWS, 2 * ROWS), 2 * ROWS), :].astype(f32)
        w_ref[pl.ds(i * PITCH, ROWS), :] = ctf * rows[:ROWS]
        w_ref[pl.ds(i * PITCH + ROWS, ROWS), :] = ctf * rows[ROWS:]
        return carry

    return weigh


def half_weigher(ky_low, turns_ref, wide_ref, x_ref, w_ref):
    stays = lax.broadcasted_iota(jnp.int32, (8, LANES), 0) % 2 == ky_low
    shift = 1 if ky_low == 0 else 7

    def wanted(first, second):
        return jnp.where(stays, first, pltpu.roll(second, shift, 0))

    turns = wanted(turns_ref[0:8, :], turns_ref[8:16, :])

    def weigh(i, carry):
        ctf = contrast(turns, wide_ref[pl.ds(i, 1), :])
        rows = x_ref[pl.ds(pl.multiple_of(i * 2 * ROWS, 2 * ROWS), 2 * ROWS), :].astype(f32)
        w_ref[pl.ds(i * PITCH, 8), :] = ctf * wanted(rows[0:8], rows[8:16])
        w_ref[pl.ds(i * PITCH + ROWS, 8), :] = ctf * wanted(rows[16:24], rows[24:32])
        return carry

    return weigh


def first_kernel(planes, x_hbm, focus_hbm, pose_hbm, label_hbm, turns_hbm, bins_hbm, along_z_hbm, table_hbm,
                 out_ref, w_ref, x_ref, wide_ref, turns_ref, spread_ref, table_ref, factor_ref,
                 focus_ref, pose_ref, label_ref, bins_ref, along_z_ref, v_ref, sems):
    number = wide_ref.shape[0]
    chunk = x_ref.shape[0] // CHUNKS

    def copy(source, target, at):
        made = pltpu.make_async_copy(source, target, sems.at[at])
        made.start()
        return made

    small = [
        copy(source, target, at)
        for at, (source, target) in enumerate(
            (
                (focus_hbm, focus_ref),
                (turns_hbm, turns_ref),
                (pose_hbm, pose_ref),
                (label_hbm, label_ref),
                (bins_hbm, bins_ref),
                (along_z_hbm, along_z_ref),
            )
        )
    ]
    parts = [
        copy(x_hbm.at[pl.ds(c * chunk, chunk)], x_ref.at[pl.ds(c * chunk, chunk)], 6 + c) for c in range(CHUNKS)
    ]
    table = copy(table_hbm, table_ref, 6 + CHUNKS)
    for made in small:
        made.wait()
    core = lax.axis_index("img") % 2
    wide_ref[...] = jnp.broadcast_to(focus_ref[...].astype(f32), (LANES, number)).T
    planar = spread_matrix(pose_ref[...], label_ref[...], planes, 0)
    xbin = jnp.broadcast_to((pose_ref[...] % XBINS).astype(f32), (LANES, number)).T
    for at in range(0, 2 * NX, LANES):
        chosen = bins_ref[0:1, at : at + LANES]
        for b in range(1, XBINS):
            chosen = jnp.where(xbin == b, bins_ref[b : b + 1, at : at + LANES], chosen)
        factor_ref[:, at : at + LANES] = chosen
    full, half = weigher(turns_ref, wide_ref, x_ref, w_ref), half_weigher(1, turns_ref, wide_ref, x_ref, w_ref)
    for c in range(CHUNKS):
        parts[c].wait()
        first, last = c * number // CHUNKS, (c + 1) * number // CHUNKS

        @pl.when(core == 0)
        def _():
            lax.fori_loop(first, last, half, 0, unroll=UNROLL)

        @pl.when(core == 1)
        def _():
            lax.fori_loop(first, last, full, 0, unroll=UNROLL)

    table.wait()
    for s in range(2):
        spread = jnp.dot(along_z_ref[s], planar, preferred_element_type=f32).astype(bf16)
        spread_ref[:, s * number : (s + 1) * number] = spread
    transform(w_ref, core == 0, 1 - core, spread_ref, table_ref, factor_ref, v_ref, place(out_ref, 1 - core))


def second_kernel(w_in, x_ref, wide_ref, turns_ref, spread_ref, table_ref, factor_ref, out_ref, w_ref, v_ref):
    core = lax.axis_index("img") % 2

    @pl.when(core == 0)
    def _():
        half = half_weigher(0, turns_ref, wide_ref, x_ref, w_ref)
        lax.fori_loop(0, wide_ref.shape[0], half, 0, unroll=UNROLL)

    transform(w_ref, core == 0, core, spread_ref, table_ref, factor_ref, v_ref, place(out_ref, core))


def last_kernel(*refs):
    *got_refs, out_ref = refs
    out_ref[...] = sum(got_ref[...].astype(f32) for got_ref in got_refs)


VMEM = pl.BlockSpec(memory_space=pltpu.VMEM)
SMEM = pl.BlockSpec(memory_space=pltpu.SMEM)
HBM = pl.BlockSpec(memory_space=pltpu.HBM)


FIRST = (
    ((2, 1, 0, 3), (1, 2, 3, 0), (3, 0, 2, 1), (0, 3, 1, 2)),
    ((1, 0, 2, 3), (2, 3, 1, 0), (3, 1, 0, 2), (0, 2, 3, 1)),
)
USUAL = ((1, 2, 0, 3), (2, 1, 3, 0), (3, 0, 2, 1), (0, 3, 1, 2))
SECOND = (((1, 3, 2, 0), (2, 1, 0, 3), (3, 0, 1, 2), (0, 2, 3, 1)), USUAL, USUAL, USUAL)
FIRST_LISTED = (0, 3, 2, 1)
SECOND_LISTED = (3, 2, 1, 0)


def pairs_of(stage, slot):
    pairs = []
    for source in range(32):
        core, y, x, z = source & 1, source >> 1 & 1, source >> 2 & 1, source >> 3
        if stage == 0:
            to = FIRST[core][slot][2 * x + y]
            x, y = to >> 1, to & 1
        else:
            z = SECOND[2 * x + y][slot][z]
        pairs.append((source, z << 3 | x << 2 | y << 1 | 1 - core))
    return pairs


def ctf_weights(defocus):
    x_index = jnp.arange(NX, dtype=jnp.int32)
    signed = (x_index + NX // 2) % NX - NX // 2
    y_index = jnp.arange(KY, dtype=jnp.int32) + 1
    radius = (y_index[:, None] ** 2 + signed[None, :] ** 2).astype(f32) / float(NX * NX)
    phase = 400.0 * math.pi * defocus.astype(f32)[:, None, None] * radius[None]
    return jnp.sin(phase + 0.1)


def many_planes(images, pose_bins, labels, defocus):
    owners, groups = lax.axis_size("slab"), lax.axis_size("img")
    number = images.shape[0]
    planes = owners * 4
    weighted = (ctf_weights(defocus)[:, None] * images.astype(f32)).astype(bf16)
    table = jnp.asarray(fourier_table()).reshape(QUARTERS, LANES, 2, LANES)
    scale = 2.5 / math.sqrt(number * owners * groups * NX)
    factors = jnp.asarray(factor_table(scale)).reshape(XBINS, QUARTERS, 2, LANES)[pose_bins % XBINS]
    by_real, by_imag = (jnp.moveaxis(factors[:, :, s], 0, 1)[:, :, None] for s in range(2))
    quarters = jnp.moveaxis(weighted.astype(f32).reshape(number, 2, KY, QUARTERS, LANES), 3, 0)
    sums = quarter_sums([(part[:, 0], part[:, 1]) for part in quarters])
    sums = jnp.stack([jnp.stack(pair) for pair in sums]).astype(bf16)
    both = jnp.einsum("qrikm,qmsn->rsqikn", sums, table, preferred_element_type=f32)
    real, imag = both[0, 0] - both[1, 1], both[0, 1] + both[1, 0]
    turned = jnp.stack([real * by_real - imag * by_imag, real * by_imag + imag * by_real]).astype(bf16)
    columns = np.argsort(np.concatenate([column_of(q) for q in range(QUARTERS)]))
    turned = jnp.moveaxis(turned, 1, 3).reshape(2, number, KY, NX)[..., columns]

    def block(first_plane):
        spread = spread_matrix(pose_bins[None], labels[None], planes, first_plane)
        spread = spread.reshape(CLASSES, PLANES, number)
        return jnp.einsum("czi,sikx->kcxsz", spread, turned, preferred_element_type=f32).astype(bf16)

    parts = lax.map(block, jnp.arange(planes // PLANES, dtype=jnp.int32) * PLANES)
    parts = jnp.moveaxis(parts, 0, -2).reshape(KY, CLASSES * NX, 2, planes).astype(f32)
    total = lax.psum_scatter(parts, "img", scatter_dimension=0, tiled=True)
    total = lax.psum_scatter(total, "slab", scatter_dimension=1, tiled=True)
    table = jnp.asarray(z_table(planes).astype(np.float32)).reshape(2, 2, planes, planes)
    return jnp.einsum("yqsz,stwz->yqtw", total, table, precision=lax.Precision.HIGHEST)


def on_device(images, pose_bins, labels, defocus):
    owners, groups = lax.axis_size("slab"), lax.axis_size("img")
    number = images.shape[0]
    planes = owners * 4
    if planes != PLANES:
        return many_planes(images, pose_bins, labels, defocus)
    scale = 2.5 / math.sqrt(number * owners * groups * NX)
    x = images.reshape(number, 2, KY, QUARTERS, LANES).transpose(0, 1, 3, 2, 4).reshape(number * 2 * ROWS, LANES)
    pieces = 2 * CLASSES * QUARTERS
    w_shape = jax.ShapeDtypeStruct((number * PITCH + 40, LANES), f32)
    turns = jnp.asarray(turns_per_defocus())
    spread_shape = jax.ShapeDtypeStruct((CLASSES * 2 * PLANES, 2 * number), bf16)
    piece_shape = jax.ShapeDtypeStruct((pieces, 2 * PLANES, LANES), bf16)
    table = jnp.asarray(fourier_table())
    table_shape = jax.ShapeDtypeStruct(table.shape, bf16)
    bins = jnp.asarray(factor_table(scale))
    along_z = jnp.asarray(np.stack([np.kron(np.eye(CLASSES), part) for part in z_table(planes)]).astype(jnp.bfloat16))
    factor_shape = jax.ShapeDtypeStruct((number, 2 * NX), f32)
    work = [pltpu.VMEM((2 * number, 2 * NX), bf16)]
    other, *near = pl.pallas_call(
        functools.partial(first_kernel, planes),
        out_shape=(
            piece_shape,
            w_shape,
            jax.ShapeDtypeStruct(x.shape, bf16),
            jax.ShapeDtypeStruct((number, LANES), f32),
            jax.ShapeDtypeStruct(turns.shape, f32),
            spread_shape,
            table_shape,
            factor_shape,
        ),
        in_specs=[HBM] * 8,
        out_specs=(VMEM,) * 8,
        scratch_shapes=[
            pltpu.VMEM((1, number), bf16),
            pltpu.VMEM((1, number), jnp.int32),
            pltpu.VMEM((1, number), jnp.int32),
            pltpu.VMEM(bins.shape, f32),
            pltpu.VMEM(along_z.shape, bf16),
            *work,
            pltpu.SemaphoreType.DMA((CHUNKS + 7,)),
        ],
        compiler_params=pltpu.CompilerParams(vmem_limit_bytes=32 << 20),
        name="weigh_and_transform_other",
    )(*(
        pltpu.with_memory_space_constraint(v, pltpu.HBM)
        for v in (x, defocus[None], pose_bins[None], labels[None], turns, bins, along_z, table)
    ))
    axes = ("slab", "img")
    got = lax.ppermute(other, axes, [(i, i ^ 1) for i in range(owners * groups)])
    own, _ = pl.pallas_call(
        second_kernel,
        out_shape=(piece_shape, w_shape),
        in_specs=[VMEM] * 7,
        out_specs=(VMEM, VMEM),
        input_output_aliases={0: 1},
        scratch_shapes=work,
        compiler_params=pltpu.CompilerParams(vmem_limit_bytes=16 << 20),
        name="transform_own",
    )(*near)
    total = (own.astype(f32) + got.astype(f32)).astype(bf16)
    got = [lax.ppermute(total[4 * slot : 4 * slot + 4], axes, pairs_of(0, slot)) for slot in FIRST_LISTED]
    total = sum(g.astype(f32) for g in got).astype(bf16)
    got = [lax.ppermute(total[slot], axes, pairs_of(1, slot)) for slot in SECOND_LISTED]
    out = pl.pallas_call(
        last_kernel,
        out_shape=jax.ShapeDtypeStruct((2 * planes, LANES), f32),
        in_specs=[VMEM] * 4,
        out_specs=VMEM,
        compiler_params=pltpu.CompilerParams(vmem_limit_bytes=16 << 20),
        name="add_last",
    )(*got)
    return out.reshape(1, 2, planes, LANES).transpose(0, 3, 1, 2)


def solution(mesh):
    placed = (
        P(("slab", "img"), None, None, None),
        P(("slab", "img")),
        P(("slab", "img")),
        P(("slab", "img")),
    )
    return jax.shard_map(
        on_device, mesh=mesh, in_specs=placed, out_specs=P("img", "slab", None, None), check_vma=False
    )
```
